256 devices in a mesh: tm: 8 (over z), rows: 32 (over x, y, core).
Axes of the slice: x: 4, y: 4, z: 8, core: 2. Of those that a mesh axis runs over, the one named last changes fastest.
Arguments:
- misfit: float32 [8, 8, 512, 1024], P('tm', None, 'rows'), may hold values from -6 to 6
- multiplier_start: float32 [8, 8, 512, 1024], P('tm', None, 'rows'), may hold values from -4 to 4
- increment_start: float32 [8, 8, 512, 1024], P('tm', None, 'rows'), may hold values from -4 to 4
- obs_values: float32 [8, 8, 16384], P('tm', None, 'rows'), may hold values from -6 to 6
- obs_weights: float32 [8, 8, 16384], P('tm', None, 'rows'), may hold values from 0.5 to 2
- obs_cells: int32 [8, 16384], P('tm', 'rows'), may hold values from 0 to 16383
- wind_table: float32 [4, 2, 512, 1024], P(None, None, 'rows'), may hold values from -0.3 to 0.3
- wind_choice: int32 [8, 8], replicated, may hold values from 0 to 3
- spectrum: float32 [8, 512, 1024], P(None, None, 'rows'), may hold values from 0.2 to 2
Outputs:
- multiplier: float32 [8, 8, 512, 1024], P('tm', None, 'rows')
- increment: float32 [8, 8, 512, 1024], P('tm', None, 'rows')
The draws below stay inside these ranges and needn't reach their ends.
Inputs may be any that keep to these rules, and one draw needn't show every extreme that they name: obs_cells counts cells of the 16 x 1024 block of rows that holds its block of 512 observations; cells may repeat.
All inputs are finite; a program needn't handle non-finite values.
Results may differ from the reference program's by a relative error of at most 0.0001.
Values sent between devices are 32-bit elements; how exact they have to be, the bound alone decides.
A program may use at most 128 MiB of HBM per device.

```python
import math
import jax
import jax.numpy as jnp

NX = 1024
LEV = 8
ROW_DEV = 16
OBS_DEV = 512
NVEL = 4
ITERS = 2
NY = 512
SECT = 8
OBS = 16384


def set_ends(entries, rng, smallest, top_value):
    index_at = [jax.random.randint(jax.random.fold_in(rng, axis), (), 0, length) for axis, length in enumerate(entries.shape)]
    main_axis = entries.shape.index(max(entries.shape))
    beside = index_at[:main_axis] + [(index_at[main_axis] + 1) % entries.shape[main_axis]] + index_at[main_axis + 1:]
    return entries.at[tuple(index_at)].set(smallest).at[tuple(beside)].set(top_value)


def levels(stream_key, extent, cuts, least, top_value):
    level, own = 1.0, jax.random.fold_in(stream_key, 6)
    for position, parts in cuts:
        heights = jnp.exp(jax.random.uniform(jax.random.fold_in(own, position), (parts,), jnp.float32, least / len(cuts), top_value / len(cuts)))
        level = level * jnp.repeat(heights, extent[position] // parts).reshape([-1 if axis == position else 1 for axis in range(len(extent))])
    return level


def centred(stream_key, dims, scale, limit, split=(), kind=jnp.bfloat16):
    array = jax.random.normal(stream_key, dims, jnp.float32) * scale
    if len(split) > 0:
        array = levels(stream_key, dims, split, -0.22, 0.18) * array
    return jnp.clip(array, min=-limit, max=limit).astype(kind)


def setup_inputs(seed: int = 0) -> dict:
    key_of = jax.random.split(jax.random.key(seed), 10)
    return {
        "misfit": centred(key_of[0], (SECT, LEV, NY, NX), 1.0, 6.0, ((0, 8), (2, 32)), jnp.float32),
        "multiplier_start": centred(key_of[1], (SECT, LEV, NY, NX), 0.5, 4.0, ((0, 8), (2, 32)), jnp.float32),
        "increment_start": centred(key_of[2], (SECT, LEV, NY, NX), 0.5, 4.0, ((0, 8), (2, 32)), jnp.float32),
        "obs_values": centred(key_of[3], (SECT, LEV, OBS), 1.0, 6.0, ((0, 8), (2, 32)), jnp.float32),
        "obs_weights": jnp.clip(jnp.exp(math.log(2.0) - 1.3862944 * jax.random.uniform(key_of[4], (SECT, LEV, OBS), jnp.float32) ** levels(key_of[4], (SECT, LEV, OBS), ((0, 8), (2, 32)), -0.2, 0.2)), 0.5, 2.0),
        "obs_cells": set_ends(jax.random.randint(key_of[5], (SECT, OBS), 0, ROW_DEV * NX), jax.random.fold_in(key_of[5], 1), 0, (ROW_DEV * NX) - 1).astype(jnp.int32),
        "wind_table": jnp.clip(jax.random.uniform(key_of[6], (NVEL, 2, NY, NX), jnp.float32, -0.3, 0.3) * levels(key_of[6], (NVEL, 2, NY, NX), ((2, 32),), -0.4, 0.0), -0.3, 0.3),
        "wind_choice": set_ends(jax.random.randint(key_of[7], (SECT, LEV), 0, NVEL), jax.random.fold_in(key_of[7], 1), 0, NVEL - 1).astype(jnp.int32),
        "spectrum": jnp.clip(jnp.exp(math.log(2.0) - 2.3025851 * jax.random.uniform(key_of[8], (LEV, NY, NX), jnp.float32) ** levels(key_of[8], (LEV, NY, NX), ((2, 32),), -0.2, 0.2)), 0.2, 2.0),
    }


NU = 0.12


def forward_step(x, u, v):
    east = jnp.roll(x, -1, -1)
    west = jnp.roll(x, 1, -1)
    north = jnp.roll(x, -1, -2)
    south = jnp.roll(x, 1, -2)
    return x + NU * (east + west + north + south - 4.0 * x) - 0.5 * (u * (east - west) + v * (north - south))


def adjoint_step(x, u, v):
    east = jnp.roll(x, -1, -1)
    west = jnp.roll(x, 1, -1)
    north = jnp.roll(x, -1, -2)
    south = jnp.roll(x, 1, -2)
    along = u * x
    across = v * x
    spread = jnp.roll(along, -1, -1) - jnp.roll(along, 1, -1) + jnp.roll(across, -1, -2) - jnp.roll(across, 1, -2)
    return x + NU * (east + west + north + south - 4.0 * x) + 0.5 * spread


def hartley(field, axis):
    spectral = jnp.fft.fft(field, axis=axis)
    return jnp.real(spectral) - jnp.imag(spectral)


def covariance(field, spectrum):
    spectral = hartley(hartley(field, -1), -2) * spectrum
    return hartley(hartley(spectral, -2), -1) / (NX * NY)


def reference(misfit, multiplier_start, increment_start, obs_values, obs_weights, obs_cells, wind_table, wind_choice, spectrum):
    winds = wind_table[wind_choice]
    east_wind = winds[:, :, 0]
    north_wind = winds[:, :, 1]
    block_start = (jnp.arange(OBS, dtype=jnp.int32) // OBS_DEV) * (ROW_DEV * NX)
    cells = (obs_cells + block_start[None, :]).astype(jnp.int32)
    multiplier = multiplier_start
    increment = increment_start

    def spread_one(cell_row, values):
        return jnp.zeros((LEV, NY * NX), jnp.float32).at[:, cell_row].add(values)

    for step in range(ITERS):
        filtered = covariance(multiplier, spectrum)
        moved = forward_step(forward_step(increment, east_wind, north_wind), east_wind, north_wind)
        forward = jnp.concatenate([jnp.zeros_like(moved[:1]), moved[:-1]], axis=0)
        r_lam = misfit - filtered - increment + forward
        flat = increment.reshape(SECT, LEV, NY * NX)
        picked = jnp.take_along_axis(flat, cells[:, None, :], axis=2)
        weighted = obs_weights * (obs_values - picked)
        spread = jax.vmap(spread_one)(cells, weighted).reshape(SECT, LEV, NY, NX)
        following = jnp.concatenate([multiplier[1:], jnp.zeros_like(multiplier[:1])], axis=0)
        backward = adjoint_step(adjoint_step(following, east_wind, north_wind), east_wind, north_wind)
        r_dx = spread - multiplier + backward
        total_lam = jnp.sum(r_lam * r_lam)
        total_dx = jnp.sum(r_dx * r_dx)
        theta = total_lam / (total_lam + total_dx + 1e-6)
        multiplier = multiplier + theta * r_lam
        increment = increment + (1.0 - theta) * r_dx
    return multiplier, increment
```

```python
import functools
import math

import jax
import jax.numpy as jnp
import numpy as np
from jax import lax
from jax.experimental import pallas as pl
from jax.experimental.pallas import tpu as pltpu
from jax.sharding import PartitionSpec as P

MESH = pl.DeviceIdType.MESH
F32 = jnp.float32
BF16 = jnp.bfloat16
NU = 0.12
MID = 1.0 - 4.0 * NU
LEV = 8
ROW = 16
COL = 32


def cas_pair(length):
    count = np.arange(length)
    angle = (count[:, None] * count[None, :] % length) * (2.0 * math.pi / length)
    table = (np.cos(angle) + np.sin(angle)).astype(np.float32)
    high = table.astype(jnp.bfloat16)
    low = (table - high.astype(np.float32)).astype(jnp.bfloat16)
    return high, low


def dot(a, b):
    return lax.dot_general(a, b, (((1,), (0,)), ((), ())), preferred_element_type=F32)


def dot_t(a, b):
    return lax.dot_general(a, b, (((1,), (1,)), ((), ())), preferred_element_type=F32)


def split(x):
    high = x.astype(BF16)
    return high, (x - high.astype(F32)).astype(BF16)


def swap_blocks(tiles):
    lane = lax.broadcasted_iota(jnp.int32, tiles[0].shape, 1)
    low = lane < 64
    even = (lane // 32) % 2 == 0
    t = list(tiles)
    for i, j in ((0, 2), (1, 3)):
        a, b = t[i], t[j]
        t[i] = jnp.where(low, a, pltpu.roll(b, 64, 1))
        t[j] = jnp.where(low, pltpu.roll(a, 64, 1), b)
    for i, j in ((0, 1), (2, 3)):
        a, b = t[i], t[j]
        t[i] = jnp.where(even, a, pltpu.roll(b, 32, 1))
        t[j] = jnp.where(even, pltpu.roll(a, 96, 1), b)
    return t


def forward_pass(src, dst, count, u, v, shift, width):
    @pl.loop(0, count)
    def _(j):
        x = src[j + 1]
        xs = src[j]
        xn = src[j + 2]
        e = pltpu.roll(x, width - 1, 1)
        w = pltpu.roll(x, 1, 1)
        k = j + shift
        dst[j] = MID * x + NU * ((e + w) + (xn + xs)) - (u[k] * (e - w) + v[k] * (xn - xs))


def adjoint_pass(src, dst, count, u, v, shift, width):
    @pl.loop(0, count)
    def _(j):
        x = src[j + 1]
        xs = src[j]
        xn = src[j + 2]
        k = j + shift
        t = NU * x
        ux = u[k] * x
        e = pltpu.roll(t + ux, width - 1, 1)
        w = pltpu.roll(t - ux, 1, 1)
        dst[j] = MID * x + (e + w) + ((NU * xn + v[k + 1] * xn) + (NU * xs - v[k - 1] * xs))


def kernel(
    rows_n,
    tm_n,
    misfit_h,
    mult_h,
    inc_h,
    obs_ref,
    weight_ref,
    cells_ref,
    wind_h,
    choice_ref,
    spec_h,
    txh_h,
    txl_h,
    tyh_h,
    tyl_h,
    mult_out,
    inc_out,
    misfit_v,
    mult_v,
    inc_v,
    wind_v,
    spec_v,
    txh,
    txl,
    tyh,
    tyl,
    pm,
    pi,
    pw,
    pd,
    pr,
    own_u,
    own_v,
    prev_u,
    prev_v,
    mid,
    q0,
    zsend,
    zrecv,
    asend,
    arecv,
    freq,
    pair,
    ypair,
    spec,
    smul,
    onehot,
    wpair,
    bfield,
    ffield,
    part,
    part2,
    zsum,
    rsum,
    in_sem,
    halo_s,
    halo_r,
    z_s,
    z_r,
    a_s,
    a_r,
    sum_s,
    sum_r,
    out_sem,
):
    width = 32 * rows_n
    tall = ROW * rows_n
    groups = width // 128
    tile = min(256, width)
    ytile = min(256, tall)
    me = lax.axis_index("rows")
    sec = lax.axis_index("tm")
    up = lax.rem(me + 1, rows_n)
    down = lax.rem(me + rows_n - 1, rows_n)
    after = lax.rem(sec + 1, tm_n)
    before = lax.rem(sec + tm_n - 1, tm_n)

    class Load:
        def __init__(self, n, src, dst, grouped):
            self.n, self.dst = n, dst
            if grouped:
                for g in range(groups):
                    lanes = src.at[:, 128 * g : 128 * g + 128]
                    pltpu.make_async_copy(lanes, dst.at[g], in_sem.at[n]).start()
            else:
                pltpu.make_async_copy(src, dst, in_sem.at[n]).start()

        def wait(self):
            pltpu.make_async_copy(self.dst, self.dst, in_sem.at[self.n]).wait()

    loads = [
        Load(n, *each)
        for n, each in enumerate(
            (
                (mult_h, mult_v, True),
                (wind_h, wind_v, True),
                (inc_h, inc_v, True),
                (txh_h, txh, False),
                (txl_h, txl, False),
                (misfit_h, misfit_v, True),
                (spec_h, spec_v, False),
                (tyh_h, tyh, False),
                (tyl_h, tyl, False),
            )
        )
    ]

    barrier = pltpu.get_barrier_semaphore()

    @pl.loop(1, rows_n)
    def _(s):
        pl.semaphore_signal(
            barrier, inc=1, device_id={"rows": lax.rem(me + s, rows_n)}, device_id_type=MESH
        )

    @pl.loop(1, tm_n)
    def _(s):
        pl.semaphore_signal(
            barrier, inc=1, device_id={"tm": lax.rem(sec + s, tm_n)}, device_id_type=MESH
        )

    def regroup(src, dst):
        @pl.loop(0, ROW)
        def _(r):
            for g in range(groups):
                dst[r + 2, :, 128 * g : 128 * g + 128] = src[g, pl.ds(r, LEV, stride=ROW), :]

    loads[0].wait()
    regroup(mult_v, pm)
    loads[1].wait()
    regroup(wind_v, pw)
    loads[2].wait()
    regroup(inc_v, pi)

    pl.semaphore_wait(barrier, rows_n - 1 + tm_n - 1)

    def halo(field, n):
        to_down = pltpu.make_async_remote_copy(
            src_ref=field.at[pl.ds(2, 2)],
            dst_ref=field.at[pl.ds(18, 2)],
            send_sem=halo_s.at[2 * n],
            recv_sem=halo_r.at[2 * n],
            device_id={"rows": down},
            device_id_type=MESH,
        )
        to_up = pltpu.make_async_remote_copy(
            src_ref=field.at[pl.ds(16, 2)],
            dst_ref=field.at[pl.ds(0, 2)],
            send_sem=halo_s.at[2 * n + 1],
            recv_sem=halo_r.at[2 * n + 1],
            device_id={"rows": up},
            device_id_type=MESH,
        )
        to_down.start()
        to_up.start()
        return to_down, to_up

    def shift(n, target):
        copy = pltpu.make_async_remote_copy(
            src_ref=zsend.at[n],
            dst_ref=zrecv.at[n],
            send_sem=z_s.at[n],
            recv_sem=z_r.at[n],
            device_id={"tm": target},
            device_id_type=MESH,
        )
        copy.start()
        return copy

    def exchange(n):
        pltpu.make_async_copy(asend.at[n, me], arecv.at[n, me], a_r.at[n]).start()

        @pl.loop(1, rows_n)
        def _(s):
            other = lax.rem(me + s, rows_n)
            pltpu.make_async_remote_copy(
                src_ref=asend.at[n, other],
                dst_ref=arecv.at[n, me],
                send_sem=a_s.at[n],
                recv_sem=a_r.at[n],
                device_id={"rows": other},
                device_id_type=MESH,
            ).start()

    def arrived(n):
        pltpu.make_async_copy(arecv.at[n], arecv.at[n], a_r.at[n]).wait()

    def sent(n):
        done = asend.at[n, pl.ds(0, rows_n - 1)]
        pltpu.make_async_copy(done, done, a_s.at[n]).wait()

    def load_pair(read):
        @pl.loop(0, 8)
        def _(i):
            x = read(i)
            high, low = split(x)
            pair[pl.ds(pl.multiple_of(16 * i, 16), 16), :] = high
            pair[pl.ds(pl.multiple_of(128 + 16 * i, 16), 16), :] = low

    def times_table(store):
        @pl.loop(0, width // tile)
        def _(n):
            cols = pl.ds(pl.multiple_of(n * tile, tile), tile)
            both = dot(pair[...], txh[:, cols])
            store(n, cols, both[:128] + both[128:] + dot(pair[pl.ds(0, 128), :], txl[:, cols]))

    def to_columns(n):
        def store(t, cols, value):
            for h in range(tile // 128):
                freq[t * (tile // 128) + h] = value[:, 128 * h : 128 * h + 128]

        times_table(store)

        @pl.loop(0, groups)
        def _(g):
            for h in range(2):
                tiles = [freq[g, pl.ds(4 * h + i, ROW, stride=LEV), :] for i in range(4)]
                for j, t in enumerate(swap_blocks(tiles)):
                    asend[n, 4 * g + j, :, 128 * h : 128 * h + 128] = t

        exchange(n)

    def from_columns(n, dst):
        arrived(n)

        @pl.loop(0, groups)
        def _(g):
            for h in range(2):
                tiles = [arecv[n, 4 * g + j, :, 128 * h : 128 * h + 128] for j in range(4)]
                for i, t in enumerate(swap_blocks(tiles)):
                    freq[g, pl.ds(4 * h + i, ROW, stride=LEV), :] = t

        for g in range(groups):
            high, low = split(freq[g])
            pair[pl.ds(0, 128), 128 * g : 128 * g + 128] = high
            pair[pl.ds(128, 128), 128 * g : 128 * g + 128] = low

        def store(t, cols, value):
            dst[:, cols] = value

        times_table(store)

    def y_pair(read):
        @pl.loop(0, tall // 64)
        def _(i):
            rows = pl.ds(pl.multiple_of(64 * i, 64), 64)
            high, low = split(read(i, rows))
            ypair[rows, 0:256] = high
            ypair[rows, 256:512] = low

    def y_times(store):
        @pl.loop(0, tall // ytile)
        def _(i):
            rows = pl.ds(pl.multiple_of(i * ytile, ytile), ytile)
            both = dot(tyh[rows, :], ypair[...])
            low = dot(tyl[rows, :], ypair[:, 0:256])
            store(i, rows, both[:, 0:256] + both[:, 256:512] + low)

    def y_load(n):
        def read(i, rows):
            return arecv[n, pl.ds(4 * i, 4)].reshape(64, 256)

        y_pair(read)

    def y_back(n):
        def store(i, rows, value):
            asend[n, pl.ds(i * (ytile // ROW), ytile // ROW)] = value.reshape(ytile // ROW, ROW, 256)

        y_times(store)
        exchange(n)

    halos_w = halo(pw, 0)
    halos_i = halo(pi, 1)
    halos_m = halo(pm, 2)

    def read_m(i):
        return pm[pl.ds(2 + 2 * i, 2)].reshape(16, width)

    load_pair(read_m)
    loads[3].wait()
    loads[4].wait()
    to_columns(0)

    level = lax.broadcasted_iota(jnp.int32, (LEV, 1), 0)

    def picks(section):
        column = jnp.zeros((LEV, 1), jnp.int32)
        for l in range(LEV):
            column = jnp.where(level == l, choice_ref[section, l], column)
        return [jnp.broadcast_to(column == n, (LEV, width)) for n in range(4)]

    for copy in halos_w:
        copy.wait_recv()

    @pl.loop(0, ROW + 4)
    def _(r):
        half = 0.5 * pw[r]
        for section, u_ref, v_ref in ((sec, own_u, own_v), (before, prev_u, prev_v)):
            chosen = picks(section)
            for comp, ref in ((0, u_ref), (1, v_ref)):
                value = jnp.zeros((LEV, width), F32)
                for n in range(4):
                    row = jnp.broadcast_to(half[2 * n + comp : 2 * n + comp + 1], (LEV, width))
                    value = jnp.where(chosen[n], row, value)
                ref[r] = value

    for copy in halos_i:
        copy.wait_recv()
    forward_pass(pi, mid, ROW + 2, own_u, own_v, 1, width)
    forward_pass(mid, zsend.at[0], ROW, own_u, own_v, 2, width)
    z0 = shift(0, after)
    for copy in halos_m:
        copy.wait_recv()
    adjoint_pass(pm, mid, ROW + 2, prev_u, prev_v, 1, width)
    adjoint_pass(mid, zsend.at[1], ROW, prev_u, prev_v, 2, width)
    z1 = shift(1, before)

    cells = cells_ref[...]
    n_obs = cells.shape[1]
    obs_row = cells // width
    obs_col = lax.rem(cells, width)

    @pl.loop(0, width // 128)
    def _(i):
        base = pl.multiple_of(128 * i, 128)
        at = lax.broadcasted_iota(jnp.int32, (128, n_obs), 0) + base
        onehot[pl.ds(base, 128), :] = jnp.where(at == obs_col, 1.0, 0.0).astype(BF16)

    def gather():
        both = dot(pair[...], onehot[...])
        picked = both[:128] + both[128:]
        total = jnp.zeros((LEV, n_obs), F32)
        for r in range(ROW):
            total = total + jnp.where(obs_row == r, picked[LEV * r : LEV * r + LEV], 0.0)
        return total

    def scatter(values, store):
        for r in range(0, ROW, 2):
            x = jnp.concatenate(
                [jnp.where(obs_row == r, values, 0.0), jnp.where(obs_row == r + 1, values, 0.0)], axis=0
            )
            high, low = split(x)
            wpair[pl.ds(LEV * r, 16), :] = high
            wpair[pl.ds(128 + LEV * r, 16), :] = low

        @pl.loop(0, width // tile)
        def _(n):
            cols = pl.ds(pl.multiple_of(n * tile, tile), tile)
            both = dot_t(wpair[...], onehot[cols, :])
            store(cols, (both[:128] + both[128:]).reshape(ROW, LEV, tile))

    def read_i(i):
        return pi[pl.ds(2 + 2 * i, 2)].reshape(16, width)

    load_pair(read_i)
    weighted = weight_ref[...] * (obs_ref[...] - gather())

    def store_d(cols, value):
        pd[pl.ds(2, ROW), :, cols] = value - pm[pl.ds(2, ROW), :, cols]

    scatter(weighted, store_d)

    loads[5].wait()

    @pl.loop(0, ROW)
    def _(r):
        for g in range(groups):
            lanes = slice(128 * g, 128 * g + 128)
            q0[r, :, lanes] = misfit_v[g, pl.ds(r, LEV, stride=ROW), :] - pi[r + 2, :, lanes]

    loads[6].wait()

    @pl.loop(0, tall // 64)
    def _(i):
        rows = pl.ds(pl.multiple_of(64 * i, 64), 64)
        for h in range(2):
            spec[rows, 128 * h : 128 * h + 128] = jnp.concatenate(
                [spec_v[4 * h + l, rows, :] for l in range(4)], axis=1
            )

    whole = 1.0 / (width * tall)

    loads[7].wait()
    loads[8].wait()
    arrived(0)
    y_load(0)

    def store_sm(i, rows, value):
        smul[rows, :] = spec[rows, :] * value

    y_times(store_sm)

    def read_sm(i, rows):
        return smul[rows, :] * whole

    y_pair(read_sm)
    y_back(1)

    keep_back = jnp.where(sec < tm_n - 1, 1.0, 0.0)
    keep_front = jnp.where(sec > 0, 1.0, 0.0)
    z1.wait_recv()

    @pl.loop(0, ROW)
    def _(r):
        pd[r + 2] = pd[r + 2] + keep_back * zrecv[1, r]

    halos_d = halo(pd, 3)

    z0.wait_recv()

    @pl.loop(0, ROW)
    def _(r):
        q0[r] = q0[r] + keep_front * zrecv[0, r]

    def read_q(i):
        return q0[pl.ds(2 * i, 2)].reshape(16, width)

    load_pair(read_q)
    to_columns(2)

    for copy in halos_d:
        copy.wait_recv()
    forward_pass(pd, mid, ROW + 2, own_u, own_v, 1, width)
    forward_pass(mid, zsend.at[2], ROW, own_u, own_v, 2, width)
    z2 = shift(2, after)

    def read_d(i):
        return pd[pl.ds(2 + 2 * i, 2)].reshape(16, width)

    load_pair(read_d)

    def store_f(cols, value):
        ffield[:, :, cols] = value

    scatter(weight_ref[...] * gather(), store_f)

    from_columns(1, bfield)

    @pl.loop(0, ROW)
    def _(r):
        pr[r + 2] = q0[r] - bfield[pl.ds(pl.multiple_of(LEV * r, LEV), LEV), :]

    halos_r = halo(pr, 4)

    arrived(2)
    y_load(2)

    def store_rm(i, rows, value):
        smul[rows, :] = spec[rows, :] * (value - smul[rows, :]) * whole

    y_times(store_rm)

    def read_rm(i, rows):
        return smul[rows, :]

    y_pair(read_rm)
    y_back(3)

    for copy in halos_r:
        copy.wait_recv()
    adjoint_pass(pr, mid, ROW + 2, prev_u, prev_v, 1, width)
    adjoint_pass(mid, zsend.at[3], ROW, prev_u, prev_v, 2, width)
    z3 = shift(3, before)

    from_columns(3, bfield)
    z2.wait_recv()
    z3.wait_recv()

    def fields(r):
        a = pr[r + 2]
        b = bfield[pl.ds(pl.multiple_of(LEV * r, LEV), LEV), :]
        d = pd[r + 2]
        e = keep_front * zrecv[2, r] - d
        f = ffield[r]
        k = keep_back * zrecv[3, r] - a
        return a, b, d, e, f, k

    def fold(x):
        total = x[:, 0:128]
        for g in range(1, groups):
            total = total + x[:, 128 * g : 128 * g + 128]
        return total

    def products(r, sums):
        a, b, d, e, f, k = fields(r)
        pairs = (a, a), (b, b), (e, e), (a, b), (a, e), (b, e), (d, d), (f, f), (k, k), (d, f), (d, k), (f, k)
        return tuple(s + fold(x * y) for s, (x, y) in zip(sums, pairs))

    sums = lax.fori_loop(0, ROW, products, (jnp.zeros((LEV, 128), F32),) * 12)
    for n in range(12):
        part[pl.ds(n, 1), :] = jnp.sum(sums[n], axis=0, keepdims=True)
    part[pl.ds(12, 4), :] = jnp.zeros((4, 128), F32)

    def everywhere(own, slots, axis, here, count, n):
        pltpu.make_async_copy(own, slots.at[here], sum_r.at[n]).start()

        @pl.loop(1, count)
        def _(s):
            pltpu.make_async_remote_copy(
                src_ref=own,
                dst_ref=slots.at[here],
                send_sem=sum_s.at[n],
                recv_sem=sum_r.at[n],
                device_id={axis: lax.rem(here + s, count)},
                device_id_type=MESH,
            ).start()

        pltpu.make_async_copy(slots, slots, sum_r.at[n]).wait()
        return jnp.sum(slots[...], axis=0)

    part2[...] = everywhere(part, zsum, "tm", sec, tm_n, 0)
    total = jnp.sum(everywhere(part2, rsum, "rows", me, rows_n, 1), axis=1, keepdims=True)
    aa, bb, ee, ab, ae, be, dd, ff, kk, df, dk, fk = (total[n : n + 1] for n in range(12))
    t0 = aa / (aa + dd + 1e-6)
    s0 = 1.0 - t0
    lam = aa + t0 * t0 * bb + s0 * s0 * ee + 2.0 * (s0 * ae - t0 * ab - t0 * s0 * be)
    dx = dd + s0 * s0 * ff + t0 * t0 * kk + 2.0 * (t0 * dk - s0 * df - t0 * s0 * fk)
    lam = jnp.maximum(lam, 0.0)
    dx = jnp.maximum(dx, 0.0)
    t1 = lam / (lam + dx + 1e-6)
    s1 = 1.0 - t1

    @pl.loop(0, ROW)
    def _(r):
        a, b, d, e, f, k = fields(r)
        x = pm[r + 2] + t0 * a + t1 * (a - t0 * b + s0 * e)
        y = pi[r + 2] + s0 * d + s1 * (d - s0 * f + t0 * k)
        for g in range(groups):
            lanes = slice(128 * g, 128 * g + 128)
            mult_v[g, pl.ds(r, LEV, stride=ROW), :] = x[:, lanes]
            inc_v[g, pl.ds(r, LEV, stride=ROW), :] = y[:, lanes]

    for n, (src, dst) in enumerate(((mult_v, mult_out), (inc_v, inc_out))):
        for g in range(groups):
            lanes = dst.at[:, 128 * g : 128 * g + 128]
            pltpu.make_async_copy(src.at[g], lanes, out_sem.at[n]).start()
    for n, dst in enumerate((mult_out, inc_out)):
        pltpu.make_async_copy(dst, dst, out_sem.at[n]).wait()

    for pairs in (halos_w, halos_i, halos_m, halos_d, halos_r, (z0, z1, z2, z3)):
        for copy in pairs:
            copy.wait_send()
    for n in range(4):
        sent(n)
    gone = zsum.at[pl.ds(0, tm_n - 1)]
    pltpu.make_async_copy(gone, gone, sum_s.at[0]).wait()
    gone = rsum.at[pl.ds(0, rows_n - 1)]
    pltpu.make_async_copy(gone, gone, sum_s.at[1]).wait()


def solution(mesh):
    rows_n = mesh.shape["rows"]
    tm_n = mesh.shape["tm"]
    width = COL * rows_n
    tall = ROW * rows_n
    x_tables = cas_pair(width)
    y_tables = cas_pair(tall)

    def on_device(misfit, mult, inc, obs, weights, cells, wind, choice, spectrum):
        n_obs = cells.shape[1]
        field = (LEV * ROW, width)
        padded = (ROW + 4, LEV, width)
        lanes = (width // 128, LEV * ROW, 128)
        vm = pltpu.VMEM
        dma = pltpu.SemaphoreType.DMA
        scratch = [
            vm(lanes, F32),
            vm(lanes, F32),
            vm(lanes, F32),
            vm(lanes, F32),
            vm((LEV, tall, COL), F32),
            vm((width, width), BF16),
            vm((width, width), BF16),
            vm((tall, tall), BF16),
            vm((tall, tall), BF16),
        ]
        scratch += [vm(padded, F32)] * 9
        scratch += [
            vm((ROW + 2, LEV, width), F32),
            vm((ROW, LEV, width), F32),
            vm((4, ROW, LEV, width), F32),
            vm((4, ROW, LEV, width), F32),
            vm((4, rows_n, ROW, LEV * COL), F32),
            vm((4, rows_n, ROW, LEV * COL), F32),
            vm((width // 128, 128, 128), F32),
            vm((256, width), BF16),
            vm((tall, 512), BF16),
            vm((tall, 256), F32),
            vm((tall, 256), F32),
            vm((width, n_obs), BF16),
            vm((256, n_obs), BF16),
            vm(field, F32),
            vm((ROW, LEV, width), F32),
            vm((16, 128), F32),
            vm((16, 128), F32),
            vm((tm_n, 16, 128), F32),
            vm((rows_n, 16, 128), F32),
            dma((9,)),
            dma((10,)),
            dma((10,)),
            dma((4,)),
            dma((4,)),
            dma((4,)),
            dma((4,)),
            dma((2,)),
            dma((2,)),
            dma((2,)),
        ]
        anywhere = pl.BlockSpec(memory_space=pl.ANY)
        near = pl.BlockSpec(memory_space=pltpu.VMEM)
        outs = pl.pallas_call(
            functools.partial(kernel, rows_n, tm_n),
            out_shape=(jax.ShapeDtypeStruct(field, F32),) * 2,
            in_specs=[
                anywhere,
                anywhere,
                anywhere,
                near,
                near,
                near,
                anywhere,
                pl.BlockSpec(memory_space=pltpu.SMEM),
                anywhere,
                anywhere,
                anywhere,
                anywhere,
                anywhere,
            ],
            out_specs=(anywhere, anywhere),
            scratch_shapes=scratch,
            compiler_params=pltpu.CompilerParams(
                collective_id=0, has_side_effects=True, vmem_limit_bytes=56 * 1024 * 1024
            ),
            name="saddle",
        )(
            misfit.reshape(field),
            mult.reshape(field),
            inc.reshape(field),
            obs[0],
            weights[0],
            cells,
            wind.reshape(field),
            choice,
            spectrum,
            *(jnp.asarray(t) for t in x_tables),
            *(jnp.asarray(t) for t in y_tables),
        )
        return tuple(o.reshape(1, LEV, ROW, width) for o in outs)

    return jax.shard_map(
        on_device,
        mesh=mesh,
        in_specs=(
            P("tm", None, "rows", None),
            P("tm", None, "rows", None),
            P("tm", None, "rows", None),
            P("tm", None, "rows"),
            P("tm", None, "rows"),
            P("tm", "rows"),
            P(None, None, "rows", None),
            P(),
            P(None, None, "rows"),
        ),
        out_specs=(P("tm", None, "rows", None), P("tm", None, "rows", None)),
        check_vma=False,
    )
```

```python
import functools
import math

import jax
import jax.numpy as jnp
import numpy as np
from jax import lax
from jax.experimental import pallas as pl
from jax.experimental.pallas import tpu as pltpu
from jax.sharding import PartitionSpec as P

MESH = pl.DeviceIdType.MESH
F32 = jnp.float32
BF16 = jnp.bfloat16
NU = 0.12
MID = 1.0 - 4.0 * NU
LEV = 8
ROW = 16
COL = 32


def cas_pair(length):
    count = np.arange(length)
    angle = (count[:, None] * count[None, :] % length) * (2.0 * math.pi / length)
    table = (np.cos(angle) + np.sin(angle)).astype(np.float32)
    high = table.astype(jnp.bfloat16)
    low = (table - high.astype(np.float32)).astype(jnp.bfloat16)
    return high, low


def dot(a, b):
    return lax.dot_general(a, b, (((1,), (0,)), ((), ())), preferred_element_type=F32)


def dot_t(a, b):
    return lax.dot_general(a, b, (((1,), (1,)), ((), ())), preferred_element_type=F32)


def split(x):
    high = x.astype(BF16)
    return high, (x - high.astype(F32)).astype(BF16)


def swap_blocks(tiles):
    lane = lax.broadcasted_iota(jnp.int32, tiles[0].shape, 1)
    low = lane < 64
    even = (lane // 32) % 2 == 0
    t = list(tiles)
    for i, j in ((0, 2), (1, 3)):
        a, b = t[i], t[j]
        t[i] = jnp.where(low, a, pltpu.roll(b, 64, 1))
        t[j] = jnp.where(low, pltpu.roll(a, 64, 1), b)
    for i, j in ((0, 1), (2, 3)):
        a, b = t[i], t[j]
        t[i] = jnp.where(even, a, pltpu.roll(b, 32, 1))
        t[j] = jnp.where(even, pltpu.roll(a, 96, 1), b)
    return t


def forward_pass(src, store, first, last, u, v, shift, width):
    @pl.loop(first, last, unroll=2)
    def _(j):
        x = src[j + 1]
        xs = src[j]
        xn = src[j + 2]
        e = pltpu.roll(x, width - 1, 1)
        w = pltpu.roll(x, 1, 1)
        k = j + shift
        store(j, MID * x + NU * ((e + w) + (xn + xs)) - (u[k] * (e - w) + v[k] * (xn - xs)))


def adjoint_pass(src, store, first, last, u, v, shift, width):
    @pl.loop(first, last, unroll=2)
    def _(j):
        x = src[j + 1]
        xs = src[j]
        xn = src[j + 2]
        k = j + shift
        t = NU * x
        ux = u[k] * x
        e = pltpu.roll(t + ux, width - 1, 1)
        w = pltpu.roll(t - ux, 1, 1)
        store(j, MID * x + (e + w) + ((NU * xn + v[k + 1] * xn) + (NU * xs - v[k - 1] * xs)))


def kernel(
    rows_n,
    tm_n,
    misfit_h,
    mult_h,
    inc_h,
    obs_ref,
    weight_ref,
    cells_ref,
    wind_h,
    choice_ref,
    spec_h,
    txh_h,
    txl_h,
    tyh_h,
    tyl_h,
    mult_out,
    inc_out,
    misfit_v,
    mult_v,
    inc_v,
    wind_v,
    spec_v,
    txh,
    txl,
    tyh,
    tyl,
    pm,
    pi,
    pw,
    pd,
    pr,
    own_u,
    own_v,
    prev_u,
    prev_v,
    mid,
    q0,
    xi,
    xm,
    xd,
    xr,
    efield,
    kfield,
    asend,
    arecv,
    freq,
    pair,
    ypair,
    spec,
    smul,
    onehot,
    wpair,
    bfield,
    ffield,
    part,
    part2,
    zsum,
    rsum,
    in_sem,
    halo_s,
    halo_r,
    z_s,
    z_r,
    a_s,
    a_r,
    sum_s,
    sum_r,
    out_sem,
):
    width = 32 * rows_n
    tall = ROW * rows_n
    groups = width // 128
    tile = min(256, width)
    ytile = min(256, tall)
    me = lax.axis_index("rows")
    sec = lax.axis_index("tm")
    up = lax.rem(me + 1, rows_n)
    down = lax.rem(me + rows_n - 1, rows_n)
    after = lax.rem(sec + 1, tm_n)
    before = lax.rem(sec + tm_n - 1, tm_n)

    barrier = pltpu.get_barrier_semaphore()

    @pl.loop(1, rows_n)
    def _(s):
        pl.semaphore_signal(
            barrier, inc=1, device_id={"rows": lax.rem(me + s, rows_n)}, device_id_type=MESH
        )

    @pl.loop(1, tm_n)
    def _(s):
        pl.semaphore_signal(
            barrier, inc=1, device_id={"tm": lax.rem(sec + s, tm_n)}, device_id_type=MESH
        )

    class Load:
        def __init__(self, n, src, dst, grouped):
            self.n, self.dst = n, dst
            if grouped:
                for g in range(groups):
                    lanes = src.at[:, 128 * g : 128 * g + 128]
                    pltpu.make_async_copy(lanes, dst.at[g], in_sem.at[n]).start()
            else:
                pltpu.make_async_copy(src, dst, in_sem.at[n]).start()

        def wait(self):
            pltpu.make_async_copy(self.dst, self.dst, in_sem.at[self.n]).wait()

    loads = [
        Load(n, *each)
        for n, each in enumerate(
            (
                (mult_h, mult_v, True),
                (txh_h, txh, False),
                (txl_h, txl, False),
                (wind_h, wind_v, True),
                (inc_h, inc_v, True),
                (misfit_h, misfit_v, True),
                (spec_h, spec_v, False),
                (tyh_h, tyh, False),
                (tyl_h, tyl, False),
            )
        )
    ]

    def regroup(src, dst, first):
        @pl.loop(0, ROW)
        def _(r):
            for g in range(groups):
                dst[r + first, :, 128 * g : 128 * g + 128] = src[g, pl.ds(r, LEV, stride=ROW), :]

    def halo(field, n):
        to_down = pltpu.make_async_remote_copy(
            src_ref=field.at[pl.ds(2, 2)],
            dst_ref=field.at[pl.ds(18, 2)],
            send_sem=halo_s.at[2 * n],
            recv_sem=halo_r.at[2 * n],
            device_id={"rows": down},
            device_id_type=MESH,
        )
        to_up = pltpu.make_async_remote_copy(
            src_ref=field.at[pl.ds(16, 2)],
            dst_ref=field.at[pl.ds(0, 2)],
            send_sem=halo_s.at[2 * n + 1],
            recv_sem=halo_r.at[2 * n + 1],
            device_id={"rows": up},
            device_id_type=MESH,
        )
        to_down.start()
        to_up.start()
        return to_down, to_up

    def shift(src, dst, n, target):
        for first, count, sem in ((0, 2, 0), (14, 2, 0), (2, 8, 1), (10, 4, 2)):
            pltpu.make_async_remote_copy(
                src_ref=src.at[pl.ds(first, count)],
                dst_ref=dst.at[pl.ds(2 + first, count)],
                send_sem=z_s.at[n],
                recv_sem=z_r.at[n, sem],
                device_id={"tm": target},
                device_id_type=MESH,
            ).start()

    def edges(dst, n):
        rows = dst.at[pl.ds(0, 4)]
        pltpu.make_async_copy(rows, rows, z_r.at[n, 0]).wait()
        return halo(dst, n + 1)

    def front(dst, n, halos):
        rows = dst.at[pl.ds(4, 8)]
        pltpu.make_async_copy(rows, rows, z_r.at[n, 1]).wait()
        for copy in halos:
            copy.wait_recv()

    def back(dst, n):
        rows = dst.at[pl.ds(12, 4)]
        pltpu.make_async_copy(rows, rows, z_r.at[n, 2]).wait()

    def twice(one_pass, src, store, u, v, half):
        def store_mid(j, value):
            mid[j] = value

        one_pass(src, store_mid, 10 * half, 10 + 8 * half, u, v, 1, width)
        one_pass(mid, store, 8 * half, 8 + 8 * half, u, v, 2, width)

    def exchange(n, rows=slice(None)):
        pltpu.make_async_copy(asend.at[n, me, rows], arecv.at[n, me, rows], a_r.at[n]).start()

        @pl.loop(1, rows_n)
        def _(s):
            other = lax.rem(me + s, rows_n)
            pltpu.make_async_remote_copy(
                src_ref=asend.at[n, other, rows],
                dst_ref=arecv.at[n, me, rows],
                send_sem=a_s.at[n],
                recv_sem=a_r.at[n],
                device_id={"rows": other},
                device_id_type=MESH,
            ).start()

    def arrived(n):
        pltpu.make_async_copy(arecv.at[n], arecv.at[n], a_r.at[n]).wait()

    def sent(n):
        done = asend.at[n, pl.ds(0, rows_n - 1)]
        pltpu.make_async_copy(done, done, a_s.at[n]).wait()

    def load_pair(read):
        @pl.loop(0, 8)
        def _(i):
            x = read(i)
            high, low = split(x)
            pair[pl.ds(pl.multiple_of(16 * i, 16), 16), :] = high
            pair[pl.ds(pl.multiple_of(128 + 16 * i, 16), 16), :] = low

    def times_table(store):
        @pl.loop(0, width // tile)
        def _(n):
            cols = pl.ds(pl.multiple_of(n * tile, tile), tile)
            both = dot(pair[...], txh[:, cols])
            store(n, cols, both[:128] + both[128:] + dot(pair[pl.ds(0, 128), :], txl[:, cols]))

    def to_columns(n):
        def store(t, cols, value):
            for h in range(tile // 128):
                freq[t * (tile // 128) + h] = value[:, 128 * h : 128 * h + 128]

        times_table(store)

        @pl.loop(0, groups)
        def _(g):
            for h in range(2):
                tiles = [freq[g, pl.ds(4 * h + i, ROW, stride=LEV), :] for i in range(4)]
                for j, t in enumerate(swap_blocks(tiles)):
                    asend[n, 4 * g + j, :, 128 * h : 128 * h + 128] = t

    def half_to_columns(n, read, half):
        @pl.loop(0, 4)
        def _(i):
            high, low = split(read(4 * half + i))
            pair[pl.ds(pl.multiple_of(128 * half + 16 * i, 16), 16), :] = high
            pair[pl.ds(pl.multiple_of(128 * half + 64 + 16 * i, 16), 16), :] = low

        @pl.loop(0, width // tile)
        def _(t):
            cols = pl.ds(pl.multiple_of(t * tile, tile), tile)
            both = dot(pair[pl.ds(128 * half, 128), :], txh[:, cols])
            value = both[:64] + both[64:] + dot(pair[pl.ds(128 * half, 64), :], txl[:, cols])
            for h in range(tile // 128):
                freq[t * (tile // 128) + h, pl.ds(64 * half, 64)] = value[:, 128 * h : 128 * h + 128]

        @pl.loop(0, groups)
        def _(g):
            for h in range(2):
                tiles = [freq[g, pl.ds(64 * half + 4 * h + i, 8, stride=LEV), :] for i in range(4)]
                for j, t in enumerate(swap_blocks(tiles)):
                    asend[n, 4 * g + j, 8 * half : 8 * half + 8, 128 * h : 128 * h + 128] = t

        exchange(n, pl.ds(8 * half, 8))

    def from_columns(n, dst):
        arrived(n)

        @pl.loop(0, groups)
        def _(g):
            for h in range(2):
                tiles = [arecv[n, 4 * g + j, :, 128 * h : 128 * h + 128] for j in range(4)]
                for i, t in enumerate(swap_blocks(tiles)):
                    freq[g, pl.ds(4 * h + i, ROW, stride=LEV), :] = t

        for g in range(groups):
            high, low = split(freq[g])
            pair[pl.ds(0, 128), 128 * g : 128 * g + 128] = high
            pair[pl.ds(128, 128), 128 * g : 128 * g + 128] = low

        def store(t, cols, value):
            dst[:, cols] = value

        times_table(store)

    def y_pair(read):
        @pl.loop(0, tall // 64)
        def _(i):
            rows = pl.ds(pl.multiple_of(64 * i, 64), 64)
            high, low = split(read(i, rows))
            ypair[rows, 0:256] = high
            ypair[rows, 256:512] = low

    def y_times(store):
        @pl.loop(0, tall // ytile)
        def _(i):
            rows = pl.ds(pl.multiple_of(i * ytile, ytile), ytile)
            both = dot(tyh[rows, :], ypair[...])
            low = dot(tyl[rows, :], ypair[:, 0:256])
            store(i, rows, both[:, 0:256] + both[:, 256:512] + low)

    def y_load(n):
        def read(i, rows):
            return arecv[n, pl.ds(4 * i, 4)].reshape(64, 256)

        y_pair(read)

    def y_back(n):
        def store(i, rows, value):
            asend[n, pl.ds(i * (ytile // ROW), ytile // ROW)] = value.reshape(ytile // ROW, ROW, 256)

        y_times(store)
        exchange(n)

    def read_m(i):
        return pm[pl.ds(2 * i, 2)].reshape(16, width)

    loads[0].wait()
    regroup(mult_v, pm, 0)
    load_pair(read_m)
    loads[1].wait()
    loads[2].wait()
    to_columns(0)
    loads[3].wait()
    regroup(wind_v, pw, 2)
    loads[4].wait()
    regroup(inc_v, pi, 0)

    pl.semaphore_wait(barrier, rows_n - 1 + tm_n - 1)
    halos_w = halo(pw, 0)
    exchange(0)
    shift(pi, xi, 0, after)
    shift(pm, xm, 1, before)

    cells = cells_ref[...]
    n_obs = cells.shape[1]
    obs_row = cells // width
    obs_col = lax.rem(cells, width)

    @pl.loop(0, width // 128)
    def _(i):
        base = pl.multiple_of(128 * i, 128)
        at = lax.broadcasted_iota(jnp.int32, (128, n_obs), 0) + base
        onehot[pl.ds(base, 128), :] = jnp.where(at == obs_col, 1.0, 0.0).astype(BF16)

    def gather():
        both = dot(pair[...], onehot[...])
        picked = both[:128] + both[128:]
        total = jnp.zeros((LEV, n_obs), F32)
        for r in range(ROW):
            total = total + jnp.where(obs_row == r, picked[LEV * r : LEV * r + LEV], 0.0)
        return total

    def scatter(values, store):
        for r in range(0, ROW, 2):
            x = jnp.concatenate(
                [jnp.where(obs_row == r, values, 0.0), jnp.where(obs_row == r + 1, values, 0.0)], axis=0
            )
            high, low = split(x)
            wpair[pl.ds(LEV * r, 16), :] = high
            wpair[pl.ds(128 + LEV * r, 16), :] = low

        @pl.loop(0, width // tile)
        def _(n):
            cols = pl.ds(pl.multiple_of(n * tile, tile), tile)
            both = dot_t(wpair[...], onehot[cols, :])
            store(cols, (both[:128] + both[128:]).reshape(ROW, LEV, tile))

    def read_i(i):
        return pi[pl.ds(2 * i, 2)].reshape(16, width)

    load_pair(read_i)
    weighted = weight_ref[...] * (obs_ref[...] - gather())

    def store_d(cols, value):
        pd[:, :, cols] = value - pm[:, :, cols]

    scatter(weighted, store_d)

    loads[5].wait()

    @pl.loop(0, ROW)
    def _(r):
        for g in range(groups):
            lanes = slice(128 * g, 128 * g + 128)
            q0[r, :, lanes] = misfit_v[g, pl.ds(r, LEV, stride=ROW), :] - pi[r, :, lanes]

    loads[6].wait()

    @pl.loop(0, tall // 128)
    def _(i):
        rows = pl.ds(pl.multiple_of(128 * i, 128), 128)
        for h in range(2):
            lanes = slice(128 * h, 128 * h + 128)
            spec[rows, lanes] = spec_v[lanes, rows].T

    whole = 1.0 / (width * tall)

    level = lax.broadcasted_iota(jnp.int32, (LEV, 1), 0)

    def picks(section):
        column = jnp.zeros((LEV, 1), jnp.int32)
        for l in range(LEV):
            column = jnp.where(level == l, choice_ref[section, l], column)
        return [jnp.broadcast_to(column == n, (LEV, width)) for n in range(4)]

    for copy in halos_w:
        copy.wait_recv()

    @pl.loop(0, ROW + 4)
    def _(r):
        half = 0.5 * pw[r]
        for section, u_ref, v_ref in ((sec, own_u, own_v), (before, prev_u, prev_v)):
            chosen = picks(section)
            for comp, ref in ((0, u_ref), (1, v_ref)):
                value = jnp.zeros((LEV, width), F32)
                for n in range(4):
                    row = jnp.broadcast_to(half[2 * n + comp : 2 * n + comp + 1], (LEV, width))
                    value = jnp.where(chosen[n], row, value)
                ref[r] = value

    halos_i = edges(xi, 0)
    halos_m = edges(xm, 1)

    loads[7].wait()
    loads[8].wait()
    arrived(0)
    y_load(0)

    def store_sm(i, rows, value):
        smul[rows, :] = spec[rows, :] * value

    y_times(store_sm)

    def read_sm(i, rows):
        return smul[rows, :] * whole

    y_pair(read_sm)
    y_back(1)

    keep_back = jnp.where(sec < tm_n - 1, 1.0, 0.0)
    keep_front = jnp.where(sec > 0, 1.0, 0.0)

    def store_q(j, value):
        q0[j] = q0[j] + keep_front * value

    def read_q(i):
        return q0[pl.ds(2 * i, 2)].reshape(16, width)

    front(xi, 0, halos_i)
    twice(forward_pass, xi, store_q, prev_u, prev_v, 0)
    half_to_columns(2, read_q, 0)
    back(xi, 0)
    twice(forward_pass, xi, store_q, prev_u, prev_v, 1)
    half_to_columns(2, read_q, 1)

    def store_back(j, value):
        pd[j] = pd[j] + keep_back * value

    front(xm, 1, halos_m)
    twice(adjoint_pass, xm, store_back, own_u, own_v, 0)
    back(xm, 1)
    twice(adjoint_pass, xm, store_back, own_u, own_v, 1)
    shift(pd, xd, 2, after)

    from_columns(1, bfield)

    @pl.loop(0, ROW)
    def _(r):
        pr[r] = q0[r] - bfield[pl.ds(pl.multiple_of(LEV * r, LEV), LEV), :]

    shift(pr, xr, 3, before)

    def read_d(i):
        return pd[pl.ds(2 * i, 2)].reshape(16, width)

    load_pair(read_d)

    def store_f(cols, value):
        ffield[:, :, cols] = value

    scatter(weight_ref[...] * gather(), store_f)

    halos_d = edges(xd, 2)

    arrived(2)
    y_load(2)

    def store_rm(i, rows, value):
        smul[rows, :] = spec[rows, :] * (value - smul[rows, :]) * whole

    y_times(store_rm)

    def read_rm(i, rows):
        return smul[rows, :]

    y_pair(read_rm)
    y_back(3)

    halos_r = edges(xr, 3)

    def store_e(j, value):
        efield[j] = keep_front * value - pd[j]

    def store_k(j, value):
        kfield[j] = keep_back * value - pr[j]

    front(xd, 2, halos_d)
    twice(forward_pass, xd, store_e, prev_u, prev_v, 0)
    back(xd, 2)
    twice(forward_pass, xd, store_e, prev_u, prev_v, 1)
    front(xr, 3, halos_r)
    twice(adjoint_pass, xr, store_k, own_u, own_v, 0)
    back(xr, 3)
    twice(adjoint_pass, xr, store_k, own_u, own_v, 1)

    def fold(x):
        total = x[:, 0:128]
        for g in range(1, groups):
            total = total + x[:, 128 * g : 128 * g + 128]
        return total

    def inner(count, pairs_of):
        def step(r, sums):
            return tuple(s + fold(x * y) for s, (x, y) in zip(sums, pairs_of(r)))

        return lax.fori_loop(0, ROW, step, (jnp.zeros((LEV, 128), F32),) * count)

    def pairs_early(r):
        a, d, e, f, k = pr[r], pd[r], efield[r], ffield[r], kfield[r]
        return (a, a), (e, e), (a, e), (d, d), (f, f), (k, k), (d, f), (d, k), (f, k)

    early = inner(9, pairs_early)

    from_columns(3, bfield)

    def filtered(r):
        return bfield[pl.ds(pl.multiple_of(LEV * r, LEV), LEV), :]

    def pairs_late(r):
        b = filtered(r)
        return (b, b), (pr[r], b), (b, efield[r])

    late = inner(3, pairs_late)
    lane = lax.broadcasted_iota(jnp.int32, (1, 128), 1)
    row = jnp.zeros((1, 128), F32)
    for n, value in enumerate(early + late):
        one = jnp.sum(jnp.sum(value, axis=0, keepdims=True), axis=1, keepdims=True)
        row = jnp.where(lane == n, one, row)
    part[...] = row

    def everywhere(own, slots, axis, here, count, n):
        pltpu.make_async_copy(own, slots.at[here], sum_r.at[n]).start()

        @pl.loop(1, count)
        def _(s):
            pltpu.make_async_remote_copy(
                src_ref=own,
                dst_ref=slots.at[here],
                send_sem=sum_s.at[n],
                recv_sem=sum_r.at[n],
                device_id={axis: lax.rem(here + s, count)},
                device_id_type=MESH,
            ).start()

        pltpu.make_async_copy(slots, slots, sum_r.at[n]).wait()
        return jnp.sum(slots[...], axis=0)

    part2[...] = everywhere(part, zsum, "tm", sec, tm_n, 0)
    total = everywhere(part2, rsum, "rows", me, rows_n, 1)
    aa, ee, ae, dd, ff, kk, df, dk, fk, bb, ab, be = (total[:, n : n + 1] for n in range(12))
    t0 = aa / (aa + dd + 1e-6)
    s0 = 1.0 - t0
    lam = aa + t0 * t0 * bb + s0 * s0 * ee + 2.0 * (s0 * ae - t0 * ab - t0 * s0 * be)
    dx = dd + s0 * s0 * ff + t0 * t0 * kk + 2.0 * (t0 * dk - s0 * df - t0 * s0 * fk)
    lam = jnp.maximum(lam, 0.0)
    dx = jnp.maximum(dx, 0.0)
    t1 = lam / (lam + dx + 1e-6)
    s1 = 1.0 - t1

    @pl.loop(0, ROW)
    def _(r):
        a, b, d, e, f, k = pr[r], filtered(r), pd[r], efield[r], ffield[r], kfield[r]
        x = pm[r] + t0 * a + t1 * (a - t0 * b + s0 * e)
        y = pi[r] + s0 * d + s1 * (d - s0 * f + t0 * k)
        for g in range(groups):
            lanes = slice(128 * g, 128 * g + 128)
            mult_v[g, pl.ds(r, LEV, stride=ROW), :] = x[:, lanes]
            inc_v[g, pl.ds(r, LEV, stride=ROW), :] = y[:, lanes]

    for n, (src, dst) in enumerate(((mult_v, mult_out), (inc_v, inc_out))):
        for g in range(groups):
            lanes = dst.at[:, 128 * g : 128 * g + 128]
            pltpu.make_async_copy(src.at[g], lanes, out_sem.at[n]).start()
    for n, dst in enumerate((mult_out, inc_out)):
        pltpu.make_async_copy(dst, dst, out_sem.at[n]).wait()

    for copies in (halos_w, halos_i, halos_m, halos_d, halos_r):
        for copy in copies:
            copy.wait_send()
    for n, src in enumerate((pi, pm, pd, pr)):
        pltpu.make_async_copy(src, src, z_s.at[n]).wait()
    for n in range(4):
        sent(n)
    gone = zsum.at[pl.ds(0, tm_n - 1)]
    pltpu.make_async_copy(gone, gone, sum_s.at[0]).wait()
    gone = rsum.at[pl.ds(0, rows_n - 1)]
    pltpu.make_async_copy(gone, gone, sum_s.at[1]).wait()


def solution(mesh):
    rows_n = mesh.shape["rows"]
    tm_n = mesh.shape["tm"]
    width = COL * rows_n
    tall = ROW * rows_n
    x_tables = cas_pair(width)
    y_tables = cas_pair(tall)

    def on_device(misfit, mult, inc, obs, weights, cells, wind, choice, spectrum):
        n_obs = cells.shape[1]
        field = (LEV * ROW, width)
        padded = (ROW + 4, LEV, width)
        lanes = (width // 128, LEV * ROW, 128)
        vm = pltpu.VMEM
        dma = pltpu.SemaphoreType.DMA
        scratch = [
            vm(lanes, F32),
            vm(lanes, F32),
            vm(lanes, F32),
            vm(lanes, F32),
            vm((LEV * COL, tall), F32),
            vm((width, width), BF16),
            vm((width, width), BF16),
            vm((tall, tall), BF16),
            vm((tall, tall), BF16),
        ]
        inner = (ROW, LEV, width)
        scratch += [vm(inner, F32)] * 2 + [vm(padded, F32)] + [vm(inner, F32)] * 2
        scratch += [vm(padded, F32)] * 4
        scratch += [
            vm((ROW + 2, LEV, width), F32),
            vm(inner, F32),
        ]
        scratch += [vm(padded, F32)] * 4 + [vm(inner, F32)] * 2
        scratch += [
            vm((4, rows_n, ROW, LEV * COL), F32),
            vm((4, rows_n, ROW, LEV * COL), F32),
            vm((width // 128, 128, 128), F32),
            vm((256, width), BF16),
            vm((tall, 512), BF16),
            vm((tall, 256), F32),
            vm((tall, 256), F32),
            vm((width, n_obs), BF16),
            vm((256, n_obs), BF16),
            vm(field, F32),
            vm((ROW, LEV, width), F32),
            vm((1, 128), F32),
            vm((1, 128), F32),
            vm((tm_n, 1, 128), F32),
            vm((rows_n, 1, 128), F32),
            dma((9,)),
            dma((10,)),
            dma((10,)),
            dma((4,)),
            dma((4, 3)),
            dma((4,)),
            dma((4,)),
            dma((2,)),
            dma((2,)),
            dma((2,)),
        ]
        anywhere = pl.BlockSpec(memory_space=pl.ANY)
        near = pl.BlockSpec(memory_space=pltpu.VMEM)
        outs = pl.pallas_call(
            functools.partial(kernel, rows_n, tm_n),
            out_shape=(pltpu.VMEM(field, F32),) * 2,
            in_specs=[
                anywhere,
                anywhere,
                anywhere,
                near,
                near,
                near,
                anywhere,
                pl.BlockSpec(memory_space=pltpu.SMEM),
                anywhere,
                anywhere,
                anywhere,
                anywhere,
                anywhere,
            ],
            out_specs=(near, near),
            scratch_shapes=scratch,
            compiler_params=pltpu.CompilerParams(
                collective_id=0, has_side_effects=True, vmem_limit_bytes=56 * 1024 * 1024
            ),
            name="saddle",
        )(
            misfit.reshape(field),
            mult.reshape(field),
            inc.reshape(field),
            obs[0],
            weights[0],
            cells,
            wind.reshape(field),
            choice,
            jnp.transpose(spectrum, (0, 2, 1)).reshape(LEV * COL, tall),
            *(jnp.asarray(t) for t in x_tables),
            *(jnp.asarray(t) for t in y_tables),
        )
        return tuple(o.reshape(1, LEV, ROW, width) for o in outs)

    return jax.shard_map(
        on_device,
        mesh=mesh,
        in_specs=(
            P("tm", None, "rows", None),
            P("tm", None, "rows", None),
            P("tm", None, "rows", None),
            P("tm", None, "rows"),
            P("tm", None, "rows"),
            P("tm", "rows"),
            P(None, None, "rows", None),
            P(),
            P(None, None, "rows"),
        ),
        out_specs=(P("tm", None, "rows", None), P("tm", None, "rows", None)),
        check_vma=False,
    )
```

```python
import functools
import math

import jax
import jax.numpy as jnp
import numpy as np
from jax import lax
from jax.experimental import pallas as pl
from jax.experimental.pallas import tpu as pltpu
from jax.sharding import PartitionSpec as P

MESH = pl.DeviceIdType.MESH
F32 = jnp.float32
BF16 = jnp.bfloat16
NU = 0.12
MID = 1.0 - 4.0 * NU
LEV = 8
ROW = 16
COL = 32


def cas_pair(length):
    count = np.arange(length)
    angle = (count[:, None] * count[None, :] % length) * (2.0 * math.pi / length)
    table = (np.cos(angle) + np.sin(angle)).astype(np.float32)
    high = table.astype(jnp.bfloat16)
    low = (table - high.astype(np.float32)).astype(jnp.bfloat16)
    return high, low


def dot(a, b):
    return lax.dot_general(a, b, (((1,), (0,)), ((), ())), preferred_element_type=F32)


def dot_t(a, b):
    return lax.dot_general(a, b, (((1,), (1,)), ((), ())), preferred_element_type=F32)


def split(x):
    high = x.astype(BF16)
    return high, (x - high.astype(F32)).astype(BF16)


def swap_blocks(tiles):
    lane = lax.broadcasted_iota(jnp.int32, tiles[0].shape, 1)
    low = lane < 64
    even = (lane // 32) % 2 == 0
    t = list(tiles)
    for i, j in ((0, 2), (1, 3)):
        a, b = t[i], t[j]
        t[i] = jnp.where(low, a, pltpu.roll(b, 64, 1))
        t[j] = jnp.where(low, pltpu.roll(a, 64, 1), b)
    for i, j in ((0, 1), (2, 3)):
        a, b = t[i], t[j]
        t[i] = jnp.where(even, a, pltpu.roll(b, 32, 1))
        t[j] = jnp.where(even, pltpu.roll(a, 96, 1), b)
    return t


def forward_pass(src, store, first, last, u, v, shift, width):
    @pl.loop(first, last, unroll=4)
    def _(j):
        x = src[j + 1]
        xs = src[j]
        xn = src[j + 2]
        e = pltpu.roll(x, width - 1, 1)
        w = pltpu.roll(x, 1, 1)
        k = j + shift
        store(j, MID * x + NU * ((e + w) + (xn + xs)) - (u[k] * (e - w) + v[k] * (xn - xs)))


def adjoint_pass(src, store, first, last, u, v, shift, width):
    @pl.loop(first, last, unroll=4)
    def _(j):
        x = src[j + 1]
        xs = src[j]
        xn = src[j + 2]
        k = j + shift
        t = NU * x
        ux = u[k] * x
        e = pltpu.roll(t + ux, width - 1, 1)
        w = pltpu.roll(t - ux, 1, 1)
        store(j, MID * x + (e + w) + ((NU * xn + v[k + 1] * xn) + (NU * xs - v[k - 1] * xs)))


def kernel(
    rows_n,
    tm_n,
    misfit_h,
    mult_h,
    inc_h,
    obs_ref,
    weight_ref,
    cells_ref,
    wind_h,
    choice_ref,
    spec_h,
    txh_h,
    txl_h,
    tyh_h,
    tyl_h,
    mult_out,
    inc_out,
    misfit_v,
    mult_v,
    inc_v,
    wind_v,
    spec_v,
    txh,
    txl,
    tyh,
    tyl,
    pm,
    pi,
    pw,
    pd,
    pr,
    own_u,
    own_v,
    prev_u,
    prev_v,
    mid,
    q0,
    xi,
    xm,
    xd,
    xr,
    efield,
    kfield,
    asend,
    arecv,
    freq,
    pair,
    ypair,
    spec,
    smul,
    onehot,
    wpair,
    bfield,
    ffield,
    part,
    part2,
    zsum,
    rsum,
    in_sem,
    halo_s,
    halo_r,
    z_s,
    z_r,
    a_s,
    a_r,
    sum_s,
    sum_r,
    out_sem,
):
    width = 32 * rows_n
    tall = ROW * rows_n
    groups = width // 128
    tile = min(256, width)
    ytile = min(256, tall)
    me = lax.axis_index("rows")
    sec = lax.axis_index("tm")
    up = lax.rem(me + 1, rows_n)
    down = lax.rem(me + rows_n - 1, rows_n)
    after = lax.rem(sec + 1, tm_n)
    before = lax.rem(sec + tm_n - 1, tm_n)

    barrier = pltpu.get_barrier_semaphore()

    @pl.loop(1, rows_n)
    def _(s):
        pl.semaphore_signal(
            barrier, inc=1, device_id={"rows": lax.rem(me + s, rows_n)}, device_id_type=MESH
        )

    @pl.loop(1, tm_n)
    def _(s):
        pl.semaphore_signal(
            barrier, inc=1, device_id={"tm": lax.rem(sec + s, tm_n)}, device_id_type=MESH
        )

    class Load:
        def __init__(self, n, src, dst, grouped):
            self.n, self.dst = n, dst
            if grouped:
                for g in range(groups):
                    lanes = src.at[:, 128 * g : 128 * g + 128]
                    pltpu.make_async_copy(lanes, dst.at[g], in_sem.at[n]).start()
            else:
                pltpu.make_async_copy(src, dst, in_sem.at[n]).start()

        def wait(self):
            pltpu.make_async_copy(self.dst, self.dst, in_sem.at[self.n]).wait()

    loads = [
        Load(n, *each)
        for n, each in enumerate(
            (
                (mult_h, mult_v, True),
                (txh_h, txh, False),
                (txl_h, txl, False),
                (wind_h, wind_v, True),
                (inc_h, inc_v, True),
                (misfit_h, misfit_v, True),
                (spec_h, spec_v, False),
                (tyh_h, tyh, False),
                (tyl_h, tyl, False),
            )
        )
    ]

    def regroup(src, dst, first):
        @pl.loop(0, ROW, unroll=4)
        def _(r):
            for g in range(groups):
                dst[r + first, :, 128 * g : 128 * g + 128] = src[g, pl.ds(r, LEV, stride=ROW), :]

    def halo(field, n):
        to_down = pltpu.make_async_remote_copy(
            src_ref=field.at[pl.ds(2, 2)],
            dst_ref=field.at[pl.ds(18, 2)],
            send_sem=halo_s.at[2 * n],
            recv_sem=halo_r.at[2 * n],
            device_id={"rows": down},
            device_id_type=MESH,
        )
        to_up = pltpu.make_async_remote_copy(
            src_ref=field.at[pl.ds(16, 2)],
            dst_ref=field.at[pl.ds(0, 2)],
            send_sem=halo_s.at[2 * n + 1],
            recv_sem=halo_r.at[2 * n + 1],
            device_id={"rows": up},
            device_id_type=MESH,
        )
        to_down.start()
        to_up.start()
        return to_down, to_up

    def shift(src, dst, n, target):
        for first, count, sem in ((0, 2, 0), (14, 2, 0), (2, 8, 1), (10, 4, 2)):
            pltpu.make_async_remote_copy(
                src_ref=src.at[pl.ds(first, count)],
                dst_ref=dst.at[pl.ds(2 + first, count)],
                send_sem=z_s.at[n],
                recv_sem=z_r.at[n, sem],
                device_id={"tm": target},
                device_id_type=MESH,
            ).start()

    def edges(dst, n):
        rows = dst.at[pl.ds(0, 4)]
        pltpu.make_async_copy(rows, rows, z_r.at[n, 0]).wait()
        return halo(dst, n + 1)

    def front(dst, n, halos):
        rows = dst.at[pl.ds(4, 8)]
        pltpu.make_async_copy(rows, rows, z_r.at[n, 1]).wait()
        for copy in halos:
            copy.wait_recv()

    def back(dst, n):
        rows = dst.at[pl.ds(12, 4)]
        pltpu.make_async_copy(rows, rows, z_r.at[n, 2]).wait()

    def twice(one_pass, src, store, u, v, half):
        def store_mid(j, value):
            mid[j] = value

        one_pass(src, store_mid, 10 * half, 10 + 8 * half, u, v, 1, width)
        one_pass(mid, store, 8 * half, 8 + 8 * half, u, v, 2, width)

    def exchange(n, rows=slice(None), lanes=slice(None), sem=0):
        pltpu.make_async_copy(
            asend.at[n, me, rows, lanes], arecv.at[n, me, rows, lanes], a_r.at[n, sem]
        ).start()

        @pl.loop(1, rows_n)
        def _(s):
            other = lax.rem(me + s, rows_n)
            pltpu.make_async_remote_copy(
                src_ref=asend.at[n, other, rows, lanes],
                dst_ref=arecv.at[n, me, rows, lanes],
                send_sem=a_s.at[n],
                recv_sem=a_r.at[n, sem],
                device_id={"rows": other},
                device_id_type=MESH,
            ).start()

    def arrived(n, lanes=slice(None), sem=0):
        blocks = arecv.at[n, :, :, lanes]
        pltpu.make_async_copy(blocks, blocks, a_r.at[n, sem]).wait()

    def sent(n):
        done = asend.at[n, pl.ds(0, rows_n - 1)]
        pltpu.make_async_copy(done, done, a_s.at[n]).wait()

    def load_pair(read):
        @pl.loop(0, 8, unroll=4)
        def _(i):
            x = read(i)
            high, low = split(x)
            pair[pl.ds(pl.multiple_of(16 * i, 16), 16), :] = high
            pair[pl.ds(pl.multiple_of(128 + 16 * i, 16), 16), :] = low

    def times_table(store):
        @pl.loop(0, width // tile, unroll=2)
        def _(n):
            cols = pl.ds(pl.multiple_of(n * tile, tile), tile)
            both = dot(pair[...], txh[:, cols])
            store(n, cols, both[:128] + both[128:] + dot(pair[pl.ds(0, 128), :], txl[:, cols]))

    def to_columns(n):
        def store(t, cols, value):
            for h in range(tile // 128):
                freq[t * (tile // 128) + h] = value[:, 128 * h : 128 * h + 128]

        times_table(store)

        @pl.loop(0, groups, unroll=4)
        def _(g):
            for h in range(2):
                tiles = [freq[g, pl.ds(4 * h + i, ROW, stride=LEV), :] for i in range(4)]
                for j, t in enumerate(swap_blocks(tiles)):
                    asend[n, 4 * g + j, :, 128 * h : 128 * h + 128] = t

    def half_to_columns(n, read, half):
        @pl.loop(0, 4, unroll=4)
        def _(i):
            high, low = split(read(4 * half + i))
            pair[pl.ds(pl.multiple_of(128 * half + 16 * i, 16), 16), :] = high
            pair[pl.ds(pl.multiple_of(128 * half + 64 + 16 * i, 16), 16), :] = low

        @pl.loop(0, width // tile, unroll=2)
        def _(t):
            cols = pl.ds(pl.multiple_of(t * tile, tile), tile)
            both = dot(pair[pl.ds(128 * half, 128), :], txh[:, cols])
            value = both[:64] + both[64:] + dot(pair[pl.ds(128 * half, 64), :], txl[:, cols])
            for h in range(tile // 128):
                freq[t * (tile // 128) + h, pl.ds(64 * half, 64)] = value[:, 128 * h : 128 * h + 128]

        @pl.loop(0, groups, unroll=4)
        def _(g):
            for h in range(2):
                tiles = [freq[g, pl.ds(64 * half + 4 * h + i, 8, stride=LEV), :] for i in range(4)]
                for j, t in enumerate(swap_blocks(tiles)):
                    asend[n, 4 * g + j, 8 * half : 8 * half + 8, 128 * h : 128 * h + 128] = t

        exchange(n, pl.ds(8 * half, 8))

    def from_columns(n, dst):
        for h in range(2):
            lanes = pl.ds(128 * h, 128)
            arrived(n, lanes, h)

            @pl.loop(0, groups, unroll=4)
            def _(g):
                tiles = [arecv[n, 4 * g + j, :, lanes] for j in range(4)]
                for i, t in enumerate(swap_blocks(tiles)):
                    freq[g, pl.ds(4 * h + i, ROW, stride=LEV), :] = t

        for g in range(groups):
            high, low = split(freq[g])
            pair[pl.ds(0, 128), 128 * g : 128 * g + 128] = high
            pair[pl.ds(128, 128), 128 * g : 128 * g + 128] = low

        def store(t, cols, value):
            dst[:, cols] = value

        times_table(store)

    def y_pair(h, read):
        @pl.loop(0, tall // 64, unroll=4)
        def _(i):
            rows = pl.ds(pl.multiple_of(64 * i, 64), 64)
            high, low = split(read(i, rows, pl.ds(128 * h, 128)))
            ypair[rows, 256 * h : 256 * h + 128] = high
            ypair[rows, 256 * h + 128 : 256 * h + 256] = low

    def y_times(h, store):
        @pl.loop(0, tall // ytile, unroll=2)
        def _(i):
            rows = pl.ds(pl.multiple_of(i * ytile, ytile), ytile)
            both = dot(tyh[rows, :], ypair[:, 256 * h : 256 * h + 256])
            low = dot(tyl[rows, :], ypair[:, 256 * h : 256 * h + 128])
            store(i, rows, pl.ds(128 * h, 128), both[:, 0:128] + both[:, 128:256] + low)

    def filter_rows(came, goes, store, read):
        def read_came(i, rows, lanes):
            return arecv[came, pl.ds(4 * i, 4), :, lanes].reshape(64, 128)

        def store_back(i, rows, lanes, value):
            count = ytile // ROW
            asend[goes, pl.ds(i * count, count), :, lanes] = value.reshape(count, ROW, 128)

        arrived(came)
        for h in range(2):
            y_pair(h, read_came)
            y_times(h, store)
            y_pair(h, read)
            y_times(h, store_back)
            exchange(goes, slice(None), pl.ds(128 * h, 128), h)

    def read_m(i):
        return pm[pl.ds(2 * i, 2)].reshape(16, width)

    loads[0].wait()
    regroup(mult_v, pm, 0)
    load_pair(read_m)
    loads[1].wait()
    loads[2].wait()
    to_columns(0)
    loads[3].wait()
    regroup(wind_v, pw, 2)
    loads[4].wait()
    regroup(inc_v, pi, 0)

    pl.semaphore_wait(barrier, rows_n - 1 + tm_n - 1)
    halos_w = halo(pw, 0)
    exchange(0)
    shift(pi, xi, 0, after)
    shift(pm, xm, 1, before)

    cells = cells_ref[...]
    n_obs = cells.shape[1]
    obs_row = cells // width
    obs_col = lax.rem(cells, width)

    @pl.loop(0, width // 128, unroll=2)
    def _(i):
        base = pl.multiple_of(128 * i, 128)
        at = lax.broadcasted_iota(jnp.int32, (128, n_obs), 0) + base
        onehot[pl.ds(base, 128), :] = jnp.where(at == obs_col, 1.0, 0.0).astype(BF16)

    def gather():
        both = dot(pair[...], onehot[...])
        picked = both[:128] + both[128:]
        total = jnp.zeros((LEV, n_obs), F32)
        for r in range(ROW):
            total = total + jnp.where(obs_row == r, picked[LEV * r : LEV * r + LEV], 0.0)
        return total

    def scatter(values, store):
        for r in range(0, ROW, 2):
            x = jnp.concatenate(
                [jnp.where(obs_row == r, values, 0.0), jnp.where(obs_row == r + 1, values, 0.0)], axis=0
            )
            high, low = split(x)
            wpair[pl.ds(LEV * r, 16), :] = high
            wpair[pl.ds(128 + LEV * r, 16), :] = low

        @pl.loop(0, width // tile, unroll=2)
        def _(n):
            cols = pl.ds(pl.multiple_of(n * tile, tile), tile)
            both = dot_t(wpair[...], onehot[cols, :])
            store(cols, (both[:128] + both[128:]).reshape(ROW, LEV, tile))

    def read_i(i):
        return pi[pl.ds(2 * i, 2)].reshape(16, width)

    load_pair(read_i)
    weighted = weight_ref[...] * (obs_ref[...] - gather())

    def store_d(cols, value):
        pd[:, :, cols] = value - pm[:, :, cols]

    scatter(weighted, store_d)

    loads[5].wait()

    @pl.loop(0, ROW, unroll=4)
    def _(r):
        for g in range(groups):
            lanes = slice(128 * g, 128 * g + 128)
            q0[r, :, lanes] = misfit_v[g, pl.ds(r, LEV, stride=ROW), :] - pi[r, :, lanes]

    loads[6].wait()

    @pl.loop(0, tall // 128, unroll=2)
    def _(i):
        rows = pl.ds(pl.multiple_of(128 * i, 128), 128)
        for h in range(2):
            lanes = slice(128 * h, 128 * h + 128)
            spec[rows, lanes] = spec_v[lanes, rows].T

    whole = 1.0 / (width * tall)

    level = lax.broadcasted_iota(jnp.int32, (LEV, 1), 0)

    def picks(section):
        column = jnp.zeros((LEV, 1), jnp.int32)
        for l in range(LEV):
            column = jnp.where(level == l, choice_ref[section, l], column)
        return [jnp.broadcast_to(column == n, (LEV, width)) for n in range(4)]

    for copy in halos_w:
        copy.wait_recv()

    @pl.loop(0, ROW + 4, unroll=2)
    def _(r):
        half = 0.5 * pw[r]
        for section, u_ref, v_ref in ((sec, own_u, own_v), (before, prev_u, prev_v)):
            chosen = picks(section)
            for comp, ref in ((0, u_ref), (1, v_ref)):
                value = jnp.zeros((LEV, width), F32)
                for n in range(4):
                    row = jnp.broadcast_to(half[2 * n + comp : 2 * n + comp + 1], (LEV, width))
                    value = jnp.where(chosen[n], row, value)
                ref[r] = value

    halos_i = edges(xi, 0)
    halos_m = edges(xm, 1)

    loads[7].wait()
    loads[8].wait()

    def store_sm(i, rows, lanes, value):
        smul[rows, lanes] = spec[rows, lanes] * value

    def read_sm(i, rows, lanes):
        return smul[rows, lanes] * whole

    filter_rows(0, 1, store_sm, read_sm)

    keep_back = jnp.where(sec < tm_n - 1, 1.0, 0.0)
    keep_front = jnp.where(sec > 0, 1.0, 0.0)

    def store_q(j, value):
        q0[j] = q0[j] + keep_front * value

    def read_q(i):
        return q0[pl.ds(2 * i, 2)].reshape(16, width)

    front(xi, 0, halos_i)
    twice(forward_pass, xi, store_q, prev_u, prev_v, 0)
    half_to_columns(2, read_q, 0)
    back(xi, 0)
    twice(forward_pass, xi, store_q, prev_u, prev_v, 1)
    half_to_columns(2, read_q, 1)

    def store_back(j, value):
        pd[j] = pd[j] + keep_back * value

    front(xm, 1, halos_m)
    twice(adjoint_pass, xm, store_back, own_u, own_v, 0)
    back(xm, 1)
    twice(adjoint_pass, xm, store_back, own_u, own_v, 1)
    shift(pd, xd, 2, after)

    from_columns(1, bfield)

    @pl.loop(0, ROW, unroll=4)
    def _(r):
        pr[r] = q0[r] - bfield[pl.ds(pl.multiple_of(LEV * r, LEV), LEV), :]

    shift(pr, xr, 3, before)

    def read_d(i):
        return pd[pl.ds(2 * i, 2)].reshape(16, width)

    load_pair(read_d)

    def store_f(cols, value):
        ffield[:, :, cols] = value

    scatter(weight_ref[...] * gather(), store_f)

    halos_d = edges(xd, 2)

    def store_rm(i, rows, lanes, value):
        smul[rows, lanes] = spec[rows, lanes] * (value - smul[rows, lanes]) * whole

    def read_rm(i, rows, lanes):
        return smul[rows, lanes]

    filter_rows(2, 3, store_rm, read_rm)

    halos_r = edges(xr, 3)

    def store_e(j, value):
        efield[j] = keep_front * value - pd[j]

    def store_k(j, value):
        kfield[j] = keep_back * value - pr[j]

    front(xd, 2, halos_d)
    twice(forward_pass, xd, store_e, prev_u, prev_v, 0)
    back(xd, 2)
    twice(forward_pass, xd, store_e, prev_u, prev_v, 1)
    front(xr, 3, halos_r)
    twice(adjoint_pass, xr, store_k, own_u, own_v, 0)
    back(xr, 3)
    twice(adjoint_pass, xr, store_k, own_u, own_v, 1)

    def fold(x):
        total = x[:, 0:128]
        for g in range(1, groups):
            total = total + x[:, 128 * g : 128 * g + 128]
        return total

    def inner(count, pairs_of):
        def step(r, sums):
            return tuple(s + fold(x * y) for s, (x, y) in zip(sums, pairs_of(r)))

        return lax.fori_loop(0, ROW, step, (jnp.zeros((LEV, 128), F32),) * count)

    def pairs_early(r):
        a, d, e, f, k = pr[r], pd[r], efield[r], ffield[r], kfield[r]
        return (a, a), (e, e), (a, e), (d, d), (f, f), (k, k), (d, f), (d, k), (f, k)

    early = inner(9, pairs_early)

    from_columns(3, bfield)

    def filtered(r):
        return bfield[pl.ds(pl.multiple_of(LEV * r, LEV), LEV), :]

    def pairs_late(r):
        b = filtered(r)
        return (b, b), (pr[r], b), (b, efield[r])

    late = inner(3, pairs_late)
    lane = lax.broadcasted_iota(jnp.int32, (1, 128), 1)
    row = jnp.zeros((1, 128), F32)
    for n, value in enumerate(early + late):
        one = jnp.sum(jnp.sum(value, axis=0, keepdims=True), axis=1, keepdims=True)
        row = jnp.where(lane == n, one, row)
    part[...] = row

    def everywhere(own, slots, axis, here, count, n):
        pltpu.make_async_copy(own, slots.at[here], sum_r.at[n]).start()

        @pl.loop(1, count)
        def _(s):
            pltpu.make_async_remote_copy(
                src_ref=own,
                dst_ref=slots.at[here],
                send_sem=sum_s.at[n],
                recv_sem=sum_r.at[n],
                device_id={axis: lax.rem(here + s, count)},
                device_id_type=MESH,
            ).start()

        pltpu.make_async_copy(slots, slots, sum_r.at[n]).wait()
        return jnp.sum(slots[...], axis=0)

    part2[...] = everywhere(part, zsum, "tm", sec, tm_n, 0)
    total = everywhere(part2, rsum, "rows", me, rows_n, 1)
    aa, ee, ae, dd, ff, kk, df, dk, fk, bb, ab, be = (total[:, n : n + 1] for n in range(12))
    t0 = aa / (aa + dd + 1e-6)
    s0 = 1.0 - t0
    lam = aa + t0 * t0 * bb + s0 * s0 * ee + 2.0 * (s0 * ae - t0 * ab - t0 * s0 * be)
    dx = dd + s0 * s0 * ff + t0 * t0 * kk + 2.0 * (t0 * dk - s0 * df - t0 * s0 * fk)
    lam = jnp.maximum(lam, 0.0)
    dx = jnp.maximum(dx, 0.0)
    t1 = lam / (lam + dx + 1e-6)
    s1 = 1.0 - t1

    @pl.loop(0, ROW, unroll=4)
    def _(r):
        a, b, d, e, f, k = pr[r], filtered(r), pd[r], efield[r], ffield[r], kfield[r]
        x = pm[r] + t0 * a + t1 * (a - t0 * b + s0 * e)
        y = pi[r] + s0 * d + s1 * (d - s0 * f + t0 * k)
        for g in range(groups):
            lanes = slice(128 * g, 128 * g + 128)
            mult_v[g, pl.ds(r, LEV, stride=ROW), :] = x[:, lanes]
            inc_v[g, pl.ds(r, LEV, stride=ROW), :] = y[:, lanes]

    for n, (src, dst) in enumerate(((mult_v, mult_out), (inc_v, inc_out))):
        for g in range(groups):
            lanes = dst.at[:, 128 * g : 128 * g + 128]
            pltpu.make_async_copy(src.at[g], lanes, out_sem.at[n]).start()
    for n, dst in enumerate((mult_out, inc_out)):
        pltpu.make_async_copy(dst, dst, out_sem.at[n]).wait()

    for copies in (halos_w, halos_i, halos_m, halos_d, halos_r):
        for copy in copies:
            copy.wait_send()
    for n, src in enumerate((pi, pm, pd, pr)):
        pltpu.make_async_copy(src, src, z_s.at[n]).wait()
    for n in range(4):
        sent(n)
    gone = zsum.at[pl.ds(0, tm_n - 1)]
    pltpu.make_async_copy(gone, gone, sum_s.at[0]).wait()
    gone = rsum.at[pl.ds(0, rows_n - 1)]
    pltpu.make_async_copy(gone, gone, sum_s.at[1]).wait()


def solution(mesh):
    rows_n = mesh.shape["rows"]
    tm_n = mesh.shape["tm"]
    width = COL * rows_n
    tall = ROW * rows_n
    x_tables = cas_pair(width)
    y_tables = cas_pair(tall)

    def on_device(misfit, mult, inc, obs, weights, cells, wind, choice, spectrum):
        n_obs = cells.shape[1]
        field = (LEV * ROW, width)
        padded = (ROW + 4, LEV, width)
        lanes = (width // 128, LEV * ROW, 128)
        vm = pltpu.VMEM
        dma = pltpu.SemaphoreType.DMA
        scratch = [
            vm(lanes, F32),
            vm(lanes, F32),
            vm(lanes, F32),
            vm(lanes, F32),
            vm((LEV * COL, tall), F32),
            vm((width, width), BF16),
            vm((width, width), BF16),
            vm((tall, tall), BF16),
            vm((tall, tall), BF16),
        ]
        inner = (ROW, LEV, width)
        scratch += [vm(inner, F32)] * 2 + [vm(padded, F32)] + [vm(inner, F32)] * 2
        scratch += [vm(padded, F32)] * 4
        scratch += [
            vm((ROW + 2, LEV, width), F32),
            vm(inner, F32),
        ]
        scratch += [vm(padded, F32)] * 4 + [vm(inner, F32)] * 2
        scratch += [
            vm((4, rows_n, ROW, LEV * COL), F32),
            vm((4, rows_n, ROW, LEV * COL), F32),
            vm((width // 128, 128, 128), F32),
            vm((256, width), BF16),
            vm((tall, 512), BF16),
            vm((tall, 256), F32),
            vm((tall, 256), F32),
            vm((width, n_obs), BF16),
            vm((256, n_obs), BF16),
            vm(field, F32),
            vm((ROW, LEV, width), F32),
            vm((1, 128), F32),
            vm((1, 128), F32),
            vm((tm_n, 1, 128), F32),
            vm((rows_n, 1, 128), F32),
            dma((9,)),
            dma((10,)),
            dma((10,)),
            dma((4,)),
            dma((4, 3)),
            dma((4,)),
            dma((4, 2)),
            dma((2,)),
            dma((2,)),
            dma((2,)),
        ]
        anywhere = pl.BlockSpec(memory_space=pl.ANY)
        near = pl.BlockSpec(memory_space=pltpu.VMEM)
        outs = pl.pallas_call(
            functools.partial(kernel, rows_n, tm_n),
            out_shape=(pltpu.VMEM(field, F32),) * 2,
            in_specs=[
                anywhere,
                anywhere,
                anywhere,
                near,
                near,
                near,
                anywhere,
                pl.BlockSpec(memory_space=pltpu.SMEM),
                anywhere,
                anywhere,
                anywhere,
                anywhere,
                anywhere,
            ],
            out_specs=(near, near),
            scratch_shapes=scratch,
            compiler_params=pltpu.CompilerParams(
                collective_id=0, has_side_effects=True, vmem_limit_bytes=56 * 1024 * 1024
            ),
            name="saddle",
        )(
            misfit.reshape(field),
            mult.reshape(field),
            inc.reshape(field),
            obs[0],
            weights[0],
            cells,
            wind.reshape(field),
            choice,
            jnp.transpose(spectrum, (0, 2, 1)).reshape(LEV * COL, tall),
            *(jnp.asarray(t) for t in x_tables),
            *(jnp.asarray(t) for t in y_tables),
        )
        return tuple(o.reshape(1, LEV, ROW, width) for o in outs)

    return jax.shard_map(
        on_device,
        mesh=mesh,
        in_specs=(
            P("tm", None, "rows", None),
            P("tm", None, "rows", None),
            P("tm", None, "rows", None),
            P("tm", None, "rows"),
            P("tm", None, "rows"),
            P("tm", "rows"),
            P(None, None, "rows", None),
            P(),
            P(None, None, "rows"),
        ),
        out_specs=(P("tm", None, "rows", None), P("tm", None, "rows", None)),
        check_vma=False,
    )
```

```python
import functools
import math

import jax
import jax.numpy as jnp
import numpy as np
from jax import lax
from jax.experimental import pallas as pl
from jax.experimental.pallas import tpu as pltpu
from jax.sharding import PartitionSpec as P

MESH = pl.DeviceIdType.MESH
F32 = jnp.float32
BF16 = jnp.bfloat16
NU = 0.12
MID = 1.0 - 4.0 * NU
LEV = 8
ROW = 16
COL = 32


def cas_pair(length):
    count = np.arange(length)
    angle = (count[:, None] * count[None, :] % length) * (2.0 * math.pi / length)
    table = (np.cos(angle) + np.sin(angle)).astype(np.float32)
    high = table.astype(jnp.bfloat16)
    low = (table - high.astype(np.float32)).astype(jnp.bfloat16)
    return high, low


def dot(a, b):
    return lax.dot_general(a, b, (((1,), (0,)), ((), ())), preferred_element_type=F32)


def dot_t(a, b):
    return lax.dot_general(a, b, (((1,), (1,)), ((), ())), preferred_element_type=F32)


def split(x):
    high = x.astype(BF16)
    return high, (x - high.astype(F32)).astype(BF16)


def swap_blocks(tiles):
    lane = lax.broadcasted_iota(jnp.int32, tiles[0].shape, 1)
    low = lane < 64
    even = (lane // 32) % 2 == 0
    t = list(tiles)
    for i, j in ((0, 2), (1, 3)):
        a, b = t[i], t[j]
        t[i] = jnp.where(low, a, pltpu.roll(b, 64, 1))
        t[j] = jnp.where(low, pltpu.roll(a, 64, 1), b)
    for i, j in ((0, 1), (2, 3)):
        a, b = t[i], t[j]
        t[i] = jnp.where(even, a, pltpu.roll(b, 32, 1))
        t[j] = jnp.where(even, pltpu.roll(a, 96, 1), b)
    return t


def forward_pass(src, store, first, last, u, v, shift, width):
    @pl.loop(first, last, unroll=4)
    def _(j):
        x = src[j + 1]
        xs = src[j]
        xn = src[j + 2]
        e = pltpu.roll(x, width - 1, 1)
        w = pltpu.roll(x, 1, 1)
        k = j + shift
        store(j, MID * x + NU * ((e + w) + (xn + xs)) - (u[k] * (e - w) + v[k] * (xn - xs)))


def adjoint_pass(src, store, first, last, u, v, shift, width):
    @pl.loop(first, last, unroll=4)
    def _(j):
        x = src[j + 1]
        xs = src[j]
        xn = src[j + 2]
        k = j + shift
        t = NU * x
        ux = u[k] * x
        e = pltpu.roll(t + ux, width - 1, 1)
        w = pltpu.roll(t - ux, 1, 1)
        store(j, MID * x + (e + w) + ((NU * xn + v[k + 1] * xn) + (NU * xs - v[k - 1] * xs)))


def kernel(
    rows_n,
    tm_n,
    misfit_h,
    mult_h,
    inc_h,
    obs_ref,
    weight_ref,
    cells_ref,
    wind_h,
    choice_ref,
    spec_h,
    txh_h,
    txl_h,
    tyh_h,
    tyl_h,
    mult_out,
    inc_out,
    misfit_v,
    mult_v,
    inc_v,
    wind_v,
    spec_v,
    txh,
    txl,
    tyh,
    tyl,
    pm,
    pi,
    pw,
    pd,
    pr,
    own_u,
    own_v,
    prev_u,
    prev_v,
    mid,
    q0,
    xi,
    xm,
    xd,
    xr,
    efield,
    kfield,
    asend,
    arecv,
    freq,
    pair,
    ypair,
    spec,
    smul,
    onehot,
    wpair,
    bfield,
    ffield,
    part,
    part2,
    zsum,
    rsum,
    in_sem,
    halo_s,
    halo_r,
    z_s,
    z_r,
    a_s,
    a_r,
    sum_s,
    sum_r,
):
    width = 32 * rows_n
    tall = ROW * rows_n
    groups = width // 128
    tile = min(256, width)
    ytile = min(256, tall)
    me = lax.axis_index("rows")
    sec = lax.axis_index("tm")
    up = lax.rem(me + 1, rows_n)
    down = lax.rem(me + rows_n - 1, rows_n)
    after = lax.rem(sec + 1, tm_n)
    before = lax.rem(sec + tm_n - 1, tm_n)

    barrier = pltpu.get_barrier_semaphore()

    @pl.loop(1, rows_n)
    def _(s):
        pl.semaphore_signal(
            barrier, inc=1, device_id={"rows": lax.rem(me + s, rows_n)}, device_id_type=MESH
        )

    @pl.loop(1, tm_n)
    def _(s):
        pl.semaphore_signal(
            barrier, inc=1, device_id={"tm": lax.rem(sec + s, tm_n)}, device_id_type=MESH
        )

    class Load:
        def __init__(self, n, src, dst, grouped):
            self.n, self.dst = n, dst
            if grouped:
                for g in range(groups):
                    lanes = src.at[:, 128 * g : 128 * g + 128]
                    pltpu.make_async_copy(lanes, dst.at[g], in_sem.at[n]).start()
            else:
                pltpu.make_async_copy(src, dst, in_sem.at[n]).start()

        def wait(self):
            pltpu.make_async_copy(self.dst, self.dst, in_sem.at[self.n]).wait()

    loads = [
        Load(n, *each)
        for n, each in enumerate(
            (
                (mult_h, mult_v, True),
                (txh_h, txh, False),
                (txl_h, txl, False),
                (wind_h, wind_v, True),
                (inc_h, inc_v, True),
                (misfit_h, misfit_v, True),
                (spec_h, spec_v, False),
                (tyh_h, tyh, False),
                (tyl_h, tyl, False),
            )
        )
    ]

    def regroup(src, dst, first):
        @pl.loop(0, ROW, unroll=4)
        def _(r):
            for g in range(groups):
                dst[r + first, :, 128 * g : 128 * g + 128] = src[g, pl.ds(r, LEV, stride=ROW), :]

    def halo(field, n):
        to_down = pltpu.make_async_remote_copy(
            src_ref=field.at[pl.ds(2, 2)],
            dst_ref=field.at[pl.ds(18, 2)],
            send_sem=halo_s.at[2 * n],
            recv_sem=halo_r.at[2 * n],
            device_id={"rows": down},
            device_id_type=MESH,
        )
        to_up = pltpu.make_async_remote_copy(
            src_ref=field.at[pl.ds(16, 2)],
            dst_ref=field.at[pl.ds(0, 2)],
            send_sem=halo_s.at[2 * n + 1],
            recv_sem=halo_r.at[2 * n + 1],
            device_id={"rows": up},
            device_id_type=MESH,
        )
        to_down.start()
        to_up.start()
        return to_down, to_up

    def shift(src, dst, n, target):
        for first, count, sem in ((0, 2, 0), (14, 2, 0), (2, 8, 1), (10, 4, 2)):
            pltpu.make_async_remote_copy(
                src_ref=src.at[pl.ds(first, count)],
                dst_ref=dst.at[pl.ds(2 + first, count)],
                send_sem=z_s.at[n],
                recv_sem=z_r.at[n, sem],
                device_id={"tm": target},
                device_id_type=MESH,
            ).start()

    def edges(dst, n):
        rows = dst.at[pl.ds(0, 4)]
        pltpu.make_async_copy(rows, rows, z_r.at[n, 0]).wait()
        return halo(dst, n + 1)

    def front(dst, n, halos):
        rows = dst.at[pl.ds(4, 8)]
        pltpu.make_async_copy(rows, rows, z_r.at[n, 1]).wait()
        for copy in halos:
            copy.wait_recv()

    def back(dst, n):
        rows = dst.at[pl.ds(12, 4)]
        pltpu.make_async_copy(rows, rows, z_r.at[n, 2]).wait()

    def twice(one_pass, src, store, u, v, half):
        def store_mid(j, value):
            mid[j] = value

        one_pass(src, store_mid, 10 * half, 10 + 8 * half, u, v, 1, width)
        one_pass(mid, store, 8 * half, 8 + 8 * half, u, v, 2, width)

    def exchange(n, rows=slice(None), lanes=slice(None), sem=0):
        pltpu.make_async_copy(
            asend.at[n, me, rows, lanes], arecv.at[n, me, rows, lanes], a_r.at[n, sem]
        ).start()

        @pl.loop(1, rows_n)
        def _(s):
            other = lax.rem(me + s, rows_n)
            pltpu.make_async_remote_copy(
                src_ref=asend.at[n, other, rows, lanes],
                dst_ref=arecv.at[n, me, rows, lanes],
                send_sem=a_s.at[n],
                recv_sem=a_r.at[n, sem],
                device_id={"rows": other},
                device_id_type=MESH,
            ).start()

    def arrived(n, lanes=slice(None), sem=0):
        blocks = arecv.at[n, :, :, lanes]
        pltpu.make_async_copy(blocks, blocks, a_r.at[n, sem]).wait()

    def sent(n):
        done = asend.at[n, pl.ds(0, rows_n - 1)]
        pltpu.make_async_copy(done, done, a_s.at[n]).wait()

    def load_pair(read):
        @pl.loop(0, 8, unroll=4)
        def _(i):
            x = read(i)
            high, low = split(x)
            pair[pl.ds(pl.multiple_of(16 * i, 16), 16), :] = high
            pair[pl.ds(pl.multiple_of(128 + 16 * i, 16), 16), :] = low

    def times_table(store):
        @pl.loop(0, width // tile, unroll=2)
        def _(n):
            cols = pl.ds(pl.multiple_of(n * tile, tile), tile)
            both = dot(pair[...], txh[:, cols])
            store(n, cols, both[:128] + both[128:] + dot(pair[pl.ds(0, 128), :], txl[:, cols]))

    def to_columns(n):
        def store(t, cols, value):
            for h in range(tile // 128):
                freq[t * (tile // 128) + h] = value[:, 128 * h : 128 * h + 128]

        times_table(store)

        @pl.loop(0, groups, unroll=4)
        def _(g):
            for h in range(2):
                tiles = [freq[g, pl.ds(4 * h + i, ROW, stride=LEV), :] for i in range(4)]
                for j, t in enumerate(swap_blocks(tiles)):
                    asend[n, 4 * g + j, :, 128 * h : 128 * h + 128] = t

    def half_to_columns(n, read, half):
        @pl.loop(0, 4, unroll=4)
        def _(i):
            high, low = split(read(4 * half + i))
            pair[pl.ds(pl.multiple_of(128 * half + 16 * i, 16), 16), :] = high
            pair[pl.ds(pl.multiple_of(128 * half + 64 + 16 * i, 16), 16), :] = low

        @pl.loop(0, width // tile, unroll=2)
        def _(t):
            cols = pl.ds(pl.multiple_of(t * tile, tile), tile)
            both = dot(pair[pl.ds(128 * half, 128), :], txh[:, cols])
            value = both[:64] + both[64:] + dot(pair[pl.ds(128 * half, 64), :], txl[:, cols])
            for h in range(tile // 128):
                freq[t * (tile // 128) + h, pl.ds(64 * half, 64)] = value[:, 128 * h : 128 * h + 128]

        @pl.loop(0, groups, unroll=4)
        def _(g):
            for h in range(2):
                tiles = [freq[g, pl.ds(64 * half + 4 * h + i, 8, stride=LEV), :] for i in range(4)]
                for j, t in enumerate(swap_blocks(tiles)):
                    asend[n, 4 * g + j, 8 * half : 8 * half + 8, 128 * h : 128 * h + 128] = t

        exchange(n, pl.ds(8 * half, 8))

    def from_columns(n, dst):
        for h in range(2):
            lanes = pl.ds(128 * h, 128)
            arrived(n, lanes, h)

            @pl.loop(0, groups, unroll=4)
            def _(g):
                tiles = [arecv[n, 4 * g + j, :, lanes] for j in range(4)]
                for i, t in enumerate(swap_blocks(tiles)):
                    freq[g, pl.ds(4 * h + i, ROW, stride=LEV), :] = t

        for g in range(groups):
            high, low = split(freq[g])
            pair[pl.ds(0, 128), 128 * g : 128 * g + 128] = high
            pair[pl.ds(128, 128), 128 * g : 128 * g + 128] = low

        def store(t, cols, value):
            dst[:, cols] = value

        times_table(store)

    def y_pair(h, read):
        @pl.loop(0, tall // 64, unroll=4)
        def _(i):
            rows = pl.ds(pl.multiple_of(64 * i, 64), 64)
            high, low = split(read(i, rows, pl.ds(128 * h, 128)))
            ypair[rows, 256 * h : 256 * h + 128] = high
            ypair[rows, 256 * h + 128 : 256 * h + 256] = low

    def y_times(h, store):
        @pl.loop(0, tall // ytile, unroll=2)
        def _(i):
            rows = pl.ds(pl.multiple_of(i * ytile, ytile), ytile)
            both = dot(tyh[rows, :], ypair[:, 256 * h : 256 * h + 256])
            low = dot(tyl[rows, :], ypair[:, 256 * h : 256 * h + 128])
            store(i, rows, pl.ds(128 * h, 128), both[:, 0:128] + both[:, 128:256] + low)

    def filter_rows(came, goes, store, read):
        def read_came(i, rows, lanes):
            return arecv[came, pl.ds(4 * i, 4), :, lanes].reshape(64, 128)

        def store_back(i, rows, lanes, value):
            count = ytile // ROW
            asend[goes, pl.ds(i * count, count), :, lanes] = value.reshape(count, ROW, 128)

        arrived(came)
        for h in range(2):
            y_pair(h, read_came)
            y_times(h, store)
            y_pair(h, read)
            y_times(h, store_back)
            exchange(goes, slice(None), pl.ds(128 * h, 128), h)

    def read_m(i):
        return pm[pl.ds(2 * i, 2)].reshape(16, width)

    loads[0].wait()
    regroup(mult_v, pm, 0)
    load_pair(read_m)
    loads[1].wait()
    loads[2].wait()
    to_columns(0)
    loads[3].wait()
    regroup(wind_v, pw, 2)
    loads[4].wait()
    regroup(inc_v, pi, 0)

    pl.semaphore_wait(barrier, rows_n - 1 + tm_n - 1)
    halos_w = halo(pw, 0)
    exchange(0)
    shift(pi, xi, 0, after)

    cells = cells_ref[...]
    n_obs = cells.shape[1]
    obs_row = cells // width
    obs_col = lax.rem(cells, width)

    @pl.loop(0, width // 128, unroll=2)
    def _(i):
        base = pl.multiple_of(128 * i, 128)
        at = lax.broadcasted_iota(jnp.int32, (128, n_obs), 0) + base
        onehot[pl.ds(base, 128), :] = jnp.where(at == obs_col, 1.0, 0.0).astype(BF16)

    def gather():
        both = dot(pair[...], onehot[...])
        picked = both[:128] + both[128:]
        total = jnp.zeros((LEV, n_obs), F32)
        for r in range(ROW):
            total = total + jnp.where(obs_row == r, picked[LEV * r : LEV * r + LEV], 0.0)
        return total

    def scatter(values, store):
        for r in range(0, ROW, 2):
            x = jnp.concatenate(
                [jnp.where(obs_row == r, values, 0.0), jnp.where(obs_row == r + 1, values, 0.0)], axis=0
            )
            high, low = split(x)
            wpair[pl.ds(LEV * r, 16), :] = high
            wpair[pl.ds(128 + LEV * r, 16), :] = low

        @pl.loop(0, width // tile, unroll=2)
        def _(n):
            cols = pl.ds(pl.multiple_of(n * tile, tile), tile)
            both = dot_t(wpair[...], onehot[cols, :])
            store(cols, (both[:128] + both[128:]).reshape(ROW, LEV, tile))

    def read_i(i):
        return pi[pl.ds(2 * i, 2)].reshape(16, width)

    load_pair(read_i)
    weighted = weight_ref[...] * (obs_ref[...] - gather())

    def store_d(cols, value):
        pd[:, :, cols] = value - pm[:, :, cols]

    scatter(weighted, store_d)
    shift(pm, xm, 1, before)

    loads[5].wait()

    @pl.loop(0, ROW, unroll=4)
    def _(r):
        for g in range(groups):
            lanes = slice(128 * g, 128 * g + 128)
            q0[r, :, lanes] = misfit_v[g, pl.ds(r, LEV, stride=ROW), :] - pi[r, :, lanes]

    loads[6].wait()

    @pl.loop(0, tall // 128, unroll=2)
    def _(i):
        rows = pl.ds(pl.multiple_of(128 * i, 128), 128)
        for h in range(2):
            lanes = slice(128 * h, 128 * h + 128)
            spec[rows, lanes] = spec_v[lanes, rows].T

    whole = 1.0 / (width * tall)

    level = lax.broadcasted_iota(jnp.int32, (LEV, 1), 0)

    def picks(section):
        column = jnp.zeros((LEV, 1), jnp.int32)
        for l in range(LEV):
            column = jnp.where(level == l, choice_ref[section, l], column)
        return [jnp.broadcast_to(column == n, (LEV, width)) for n in range(4)]

    for copy in halos_w:
        copy.wait_recv()

    @pl.loop(0, ROW + 4, unroll=2)
    def _(r):
        half = 0.5 * pw[r]
        for section, u_ref, v_ref in ((sec, own_u, own_v), (before, prev_u, prev_v)):
            chosen = picks(section)
            for comp, ref in ((0, u_ref), (1, v_ref)):
                value = jnp.zeros((LEV, width), F32)
                for n in range(4):
                    row = jnp.broadcast_to(half[2 * n + comp : 2 * n + comp + 1], (LEV, width))
                    value = jnp.where(chosen[n], row, value)
                ref[r] = value

    halos_i = edges(xi, 0)
    halos_m = edges(xm, 1)

    loads[7].wait()
    loads[8].wait()

    def store_sm(i, rows, lanes, value):
        smul[rows, lanes] = spec[rows, lanes] * value

    def read_sm(i, rows, lanes):
        return smul[rows, lanes] * whole

    filter_rows(0, 1, store_sm, read_sm)

    keep_back = jnp.where(sec < tm_n - 1, 1.0, 0.0)
    keep_front = jnp.where(sec > 0, 1.0, 0.0)

    def store_q(j, value):
        q0[j] = q0[j] + keep_front * value

    def read_q(i):
        return q0[pl.ds(2 * i, 2)].reshape(16, width)

    front(xi, 0, halos_i)
    twice(forward_pass, xi, store_q, prev_u, prev_v, 0)
    half_to_columns(2, read_q, 0)
    back(xi, 0)
    twice(forward_pass, xi, store_q, prev_u, prev_v, 1)
    half_to_columns(2, read_q, 1)

    def store_back(j, value):
        pd[j] = pd[j] + keep_back * value

    front(xm, 1, halos_m)
    twice(adjoint_pass, xm, store_back, own_u, own_v, 0)
    back(xm, 1)
    twice(adjoint_pass, xm, store_back, own_u, own_v, 1)
    shift(pd, xd, 2, after)

    from_columns(1, bfield)

    @pl.loop(0, ROW, unroll=4)
    def _(r):
        pr[r] = q0[r] - bfield[pl.ds(pl.multiple_of(LEV * r, LEV), LEV), :]

    shift(pr, xr, 3, before)

    def read_d(i):
        return pd[pl.ds(2 * i, 2)].reshape(16, width)

    load_pair(read_d)

    def store_f(cols, value):
        ffield[:, :, cols] = value

    scatter(weight_ref[...] * gather(), store_f)

    halos_d = edges(xd, 2)

    def store_rm(i, rows, lanes, value):
        smul[rows, lanes] = spec[rows, lanes] * (value - smul[rows, lanes]) * whole

    def read_rm(i, rows, lanes):
        return smul[rows, lanes]

    filter_rows(2, 3, store_rm, read_rm)

    halos_r = edges(xr, 3)

    def store_e(j, value):
        efield[j] = keep_front * value - pd[j]

    def store_k(j, value):
        kfield[j] = keep_back * value - pr[j]

    front(xd, 2, halos_d)
    twice(forward_pass, xd, store_e, prev_u, prev_v, 0)
    back(xd, 2)
    twice(forward_pass, xd, store_e, prev_u, prev_v, 1)
    front(xr, 3, halos_r)
    twice(adjoint_pass, xr, store_k, own_u, own_v, 0)
    from_columns(3, bfield)
    back(xr, 3)
    twice(adjoint_pass, xr, store_k, own_u, own_v, 1)

    def fold(x):
        total = x[:, 0:128]
        for g in range(1, groups):
            total = total + x[:, 128 * g : 128 * g + 128]
        return total

    def inner(count, pairs_of):
        def step(r, sums):
            return tuple(s + fold(x * y) for s, (x, y) in zip(sums, pairs_of(r)))

        return lax.fori_loop(0, ROW, step, (jnp.zeros((LEV, 128), F32),) * count)

    def pairs_early(r):
        a, d, e, f, k = pr[r], pd[r], efield[r], ffield[r], kfield[r]
        return (a, a), (e, e), (a, e), (d, d), (f, f), (k, k), (d, f), (d, k), (f, k)

    early = inner(9, pairs_early)

    def filtered(r):
        return bfield[pl.ds(pl.multiple_of(LEV * r, LEV), LEV), :]

    def pairs_late(r):
        b = filtered(r)
        return (b, b), (pr[r], b), (b, efield[r])

    late = inner(3, pairs_late)
    lane = lax.broadcasted_iota(jnp.int32, (1, 128), 1)
    row = jnp.zeros((1, 128), F32)
    for n, value in enumerate(early + late):
        one = jnp.sum(jnp.sum(value, axis=0, keepdims=True), axis=1, keepdims=True)
        row = jnp.where(lane == n, one, row)
    part[...] = row

    def everywhere(own, slots, axis, here, count, n):
        pltpu.make_async_copy(own, slots.at[here], sum_r.at[n]).start()

        @pl.loop(1, count)
        def _(s):
            pltpu.make_async_remote_copy(
                src_ref=own,
                dst_ref=slots.at[here],
                send_sem=sum_s.at[n],
                recv_sem=sum_r.at[n],
                device_id={axis: lax.rem(here + s, count)},
                device_id_type=MESH,
            ).start()

        pltpu.make_async_copy(slots, slots, sum_r.at[n]).wait()
        return jnp.sum(slots[...], axis=0)

    part2[...] = everywhere(part, zsum, "tm", sec, tm_n, 0)
    total = everywhere(part2, rsum, "rows", me, rows_n, 1)
    aa, ee, ae, dd, ff, kk, df, dk, fk, bb, ab, be = (total[:, n : n + 1] for n in range(12))
    t0 = aa / (aa + dd + 1e-6)
    s0 = 1.0 - t0
    lam = aa + t0 * t0 * bb + s0 * s0 * ee + 2.0 * (s0 * ae - t0 * ab - t0 * s0 * be)
    dx = dd + s0 * s0 * ff + t0 * t0 * kk + 2.0 * (t0 * dk - s0 * df - t0 * s0 * fk)
    lam = jnp.maximum(lam, 0.0)
    dx = jnp.maximum(dx, 0.0)
    t1 = lam / (lam + dx + 1e-6)
    s1 = 1.0 - t1

    @pl.loop(0, ROW, unroll=4)
    def _(r):
        a, b, d, e, f, k = pr[r], filtered(r), pd[r], efield[r], ffield[r], kfield[r]
        x = pm[r] + t0 * a + t1 * (a - t0 * b + s0 * e)
        y = pi[r] + s0 * d + s1 * (d - s0 * f + t0 * k)
        for g in range(groups):
            lanes = slice(128 * g, 128 * g + 128)
            mult_v[g, pl.ds(r, LEV, stride=ROW), :] = x[:, lanes]
            inc_v[g, pl.ds(r, LEV, stride=ROW), :] = y[:, lanes]

    for g in range(groups):
        lanes = slice(128 * g, 128 * g + 128)
        mult_out[:, lanes] = mult_v[g]
        inc_out[:, lanes] = inc_v[g]

    for copies in (halos_w, halos_i, halos_m, halos_d, halos_r):
        for copy in copies:
            copy.wait_send()
    for n, src in enumerate((pi, pm, pd, pr)):
        pltpu.make_async_copy(src, src, z_s.at[n]).wait()
    for n in range(4):
        sent(n)
    gone = zsum.at[pl.ds(0, tm_n - 1)]
    pltpu.make_async_copy(gone, gone, sum_s.at[0]).wait()
    gone = rsum.at[pl.ds(0, rows_n - 1)]
    pltpu.make_async_copy(gone, gone, sum_s.at[1]).wait()


def solution(mesh):
    rows_n = mesh.shape["rows"]
    tm_n = mesh.shape["tm"]
    width = COL * rows_n
    tall = ROW * rows_n
    x_tables = cas_pair(width)
    y_tables = cas_pair(tall)

    def on_device(misfit, mult, inc, obs, weights, cells, wind, choice, spectrum):
        n_obs = cells.shape[1]
        field = (LEV * ROW, width)
        padded = (ROW + 4, LEV, width)
        lanes = (width // 128, LEV * ROW, 128)
        vm = pltpu.VMEM
        dma = pltpu.SemaphoreType.DMA
        scratch = [
            vm(lanes, F32),
            vm(lanes, F32),
            vm(lanes, F32),
            vm(lanes, F32),
            vm((LEV * COL, tall), F32),
            vm((width, width), BF16),
            vm((width, width), BF16),
            vm((tall, tall), BF16),
            vm((tall, tall), BF16),
        ]
        inner = (ROW, LEV, width)
        scratch += [vm(inner, F32)] * 2 + [vm(padded, F32)] + [vm(inner, F32)] * 2
        scratch += [vm(padded, F32)] * 4
        scratch += [
            vm((ROW + 2, LEV, width), F32),
            vm(inner, F32),
        ]
        scratch += [vm(padded, F32)] * 4 + [vm(inner, F32)] * 2
        scratch += [
            vm((4, rows_n, ROW, LEV * COL), F32),
            vm((4, rows_n, ROW, LEV * COL), F32),
            vm((width // 128, 128, 128), F32),
            vm((256, width), BF16),
            vm((tall, 512), BF16),
            vm((tall, 256), F32),
            vm((tall, 256), F32),
            vm((width, n_obs), BF16),
            vm((256, n_obs), BF16),
            vm(field, F32),
            vm((ROW, LEV, width), F32),
            vm((1, 128), F32),
            vm((1, 128), F32),
            vm((tm_n, 1, 128), F32),
            vm((rows_n, 1, 128), F32),
            dma((9,)),
            dma((10,)),
            dma((10,)),
            dma((4,)),
            dma((4, 3)),
            dma((4,)),
            dma((4, 2)),
            dma((2,)),
            dma((2,)),
        ]
        anywhere = pl.BlockSpec(memory_space=pl.ANY)
        near = pl.BlockSpec(memory_space=pltpu.VMEM)
        outs = pl.pallas_call(
            functools.partial(kernel, rows_n, tm_n),
            out_shape=(pltpu.VMEM(field, F32),) * 2,
            in_specs=[
                anywhere,
                anywhere,
                anywhere,
                near,
                near,
                near,
                anywhere,
                pl.BlockSpec(memory_space=pltpu.SMEM),
                anywhere,
                anywhere,
                anywhere,
                anywhere,
                anywhere,
            ],
            out_specs=(near, near),
            scratch_shapes=scratch,
            compiler_params=pltpu.CompilerParams(
                collective_id=0, has_side_effects=True, vmem_limit_bytes=56 * 1024 * 1024
            ),
            name="saddle",
        )(
            misfit.reshape(field),
            mult.reshape(field),
            inc.reshape(field),
            obs[0],
            weights[0],
            cells,
            wind.reshape(field),
            choice,
            jnp.transpose(spectrum, (0, 2, 1)).reshape(LEV * COL, tall),
            *(jnp.asarray(t) for t in x_tables),
            *(jnp.asarray(t) for t in y_tables),
        )
        return tuple(o.reshape(1, LEV, ROW, width) for o in outs)

    return jax.shard_map(
        on_device,
        mesh=mesh,
        in_specs=(
            P("tm", None, "rows", None),
            P("tm", None, "rows", None),
            P("tm", None, "rows", None),
            P("tm", None, "rows"),
            P("tm", None, "rows"),
            P("tm", "rows"),
            P(None, None, "rows", None),
            P(),
            P(None, None, "rows"),
        ),
        out_specs=(P("tm", None, "rows", None), P("tm", None, "rows", None)),
        check_vma=False,
    )
```

```python
import functools
import math

import jax
import jax.numpy as jnp
import numpy as np
from jax import lax
from jax.experimental import pallas as pl
from jax.experimental.pallas import tpu as pltpu
from jax.sharding import PartitionSpec as P

MESH = pl.DeviceIdType.MESH
F32 = jnp.float32
BF16 = jnp.bfloat16
NU = 0.12
MID = 1.0 - 4.0 * NU
LEV = 8
ROW = 16
COL = 32


def cas_pair(length):
    count = np.arange(length)
    angle = (count[:, None] * count[None, :] % length) * (2.0 * math.pi / length)
    table = (np.cos(angle) + np.sin(angle)).astype(np.float32)
    high = table.astype(jnp.bfloat16)
    low = (table - high.astype(np.float32)).astype(jnp.bfloat16)
    return high, low


def dot(a, b):
    return lax.dot_general(a, b, (((1,), (0,)), ((), ())), preferred_element_type=F32)


def dot_t(a, b):
    return lax.dot_general(a, b, (((1,), (1,)), ((), ())), preferred_element_type=F32)


def split(x):
    high = x.astype(BF16)
    return high, (x - high.astype(F32)).astype(BF16)


def swap_blocks(tiles):
    lane = lax.broadcasted_iota(jnp.int32, tiles[0].shape, 1)
    low = lane < 64
    even = (lane // 32) % 2 == 0
    t = list(tiles)
    for i, j in ((0, 2), (1, 3)):
        a, b = t[i], t[j]
        t[i] = jnp.where(low, a, pltpu.roll(b, 64, 1))
        t[j] = jnp.where(low, pltpu.roll(a, 64, 1), b)
    for i, j in ((0, 1), (2, 3)):
        a, b = t[i], t[j]
        t[i] = jnp.where(even, a, pltpu.roll(b, 32, 1))
        t[j] = jnp.where(even, pltpu.roll(a, 96, 1), b)
    return t


def forward_pass(src, store, first, last, u, v, shift, width):
    @pl.loop(first, last, unroll=4)
    def _(j):
        x = src[j + 1]
        xs = src[j]
        xn = src[j + 2]
        e = pltpu.roll(x, width - 1, 1)
        w = pltpu.roll(x, 1, 1)
        k = j + shift
        store(j, MID * x + NU * ((e + w) + (xn + xs)) - (u[k] * (e - w) + v[k] * (xn - xs)))


def adjoint_pass(src, store, first, last, u, v, shift, width):
    @pl.loop(first, last, unroll=4)
    def _(j):
        x = src[j + 1]
        xs = src[j]
        xn = src[j + 2]
        k = j + shift
        t = NU * x
        ux = u[k] * x
        e = pltpu.roll(t + ux, width - 1, 1)
        w = pltpu.roll(t - ux, 1, 1)
        store(j, MID * x + (e + w) + ((NU * xn + v[k + 1] * xn) + (NU * xs - v[k - 1] * xs)))


def kernel(
    rows_n,
    tm_n,
    misfit_h,
    mult_h,
    inc_h,
    obs_ref,
    weight_ref,
    cells_ref,
    wind_h,
    choice_ref,
    spec_h,
    txh_h,
    txl_h,
    tyh_h,
    tyl_h,
    mult_out,
    inc_out,
    misfit_v,
    mult_v,
    inc_v,
    wind_v,
    spec_v,
    txh,
    txl,
    tyh,
    tyl,
    pm,
    pi,
    pw,
    pd,
    pr,
    own_u,
    own_v,
    prev_u,
    prev_v,
    mid,
    q0,
    xi,
    xm,
    xd,
    xr,
    efield,
    kfield,
    asend,
    arecv,
    freq,
    pair,
    ypair,
    spec,
    smul,
    onehot,
    wpair,
    bfield,
    ffield,
    part,
    part2,
    zsum,
    rsum,
    in_sem,
    halo_s,
    halo_r,
    z_s,
    z_r,
    a_s,
    a_r,
    sum_s,
    sum_r,
):
    width = 32 * rows_n
    tall = ROW * rows_n
    groups = width // 128
    tile = min(256, width)
    ytile = min(256, tall)
    me = lax.axis_index("rows")
    sec = lax.axis_index("tm")
    up = lax.rem(me + 1, rows_n)
    down = lax.rem(me + rows_n - 1, rows_n)
    after = lax.rem(sec + 1, tm_n)
    before = lax.rem(sec + tm_n - 1, tm_n)

    barrier = pltpu.get_barrier_semaphore()

    @pl.loop(1, tm_n)
    def _(s):
        pl.semaphore_signal(
            barrier, inc=1, device_id={"tm": lax.rem(sec + s, tm_n)}, device_id_type=MESH
        )

    @pl.loop(1, rows_n)
    def _(s):
        pl.semaphore_signal(
            barrier, inc=1, device_id={"rows": lax.rem(me + s, rows_n)}, device_id_type=MESH
        )

    class Load:
        def __init__(self, n, src, dst, grouped):
            self.n, self.dst = n, dst
            if grouped:
                for g in range(groups):
                    lanes = src.at[:, 128 * g : 128 * g + 128]
                    pltpu.make_async_copy(lanes, dst.at[g], in_sem.at[n]).start()
            else:
                pltpu.make_async_copy(src, dst, in_sem.at[n]).start()

        def wait(self):
            pltpu.make_async_copy(self.dst, self.dst, in_sem.at[self.n]).wait()

    loads = [
        Load(n, *each)
        for n, each in enumerate(
            (
                (mult_h, mult_v, True),
                (txh_h, txh, False),
                (txl_h, txl, False),
                (wind_h, wind_v, True),
                (inc_h, inc_v, True),
                (misfit_h, misfit_v, True),
                (spec_h, spec_v, False),
                (tyh_h, tyh, False),
                (tyl_h, tyl, False),
            )
        )
    ]

    def regroup(src, dst, first):
        @pl.loop(0, ROW, unroll=4)
        def _(r):
            for g in range(groups):
                dst[r + first, :, 128 * g : 128 * g + 128] = src[g, pl.ds(r, LEV, stride=ROW), :]

    def halo(field, n):
        to_down = pltpu.make_async_remote_copy(
            src_ref=field.at[pl.ds(2, 2)],
            dst_ref=field.at[pl.ds(18, 2)],
            send_sem=halo_s.at[2 * n],
            recv_sem=halo_r.at[2 * n],
            device_id={"rows": down},
            device_id_type=MESH,
        )
        to_up = pltpu.make_async_remote_copy(
            src_ref=field.at[pl.ds(16, 2)],
            dst_ref=field.at[pl.ds(0, 2)],
            send_sem=halo_s.at[2 * n + 1],
            recv_sem=halo_r.at[2 * n + 1],
            device_id={"rows": up},
            device_id_type=MESH,
        )
        to_down.start()
        to_up.start()
        return to_down, to_up

    def shift(src, dst, n, target):
        for first, count, sem in ((0, 2, 0), (14, 2, 0), (2, 8, 1), (10, 4, 2)):
            pltpu.make_async_remote_copy(
                src_ref=src.at[pl.ds(first, count)],
                dst_ref=dst.at[pl.ds(2 + first, count)],
                send_sem=z_s.at[n],
                recv_sem=z_r.at[n, sem],
                device_id={"tm": target},
                device_id_type=MESH,
            ).start()

    def edges(dst, n):
        rows = dst.at[pl.ds(0, 4)]
        pltpu.make_async_copy(rows, rows, z_r.at[n, 0]).wait()
        return halo(dst, n + 1)

    def front(dst, n, halos):
        rows = dst.at[pl.ds(4, 8)]
        pltpu.make_async_copy(rows, rows, z_r.at[n, 1]).wait()
        for copy in halos:
            copy.wait_recv()

    def back(dst, n):
        rows = dst.at[pl.ds(12, 4)]
        pltpu.make_async_copy(rows, rows, z_r.at[n, 2]).wait()

    def twice(one_pass, src, store, u, v, half):
        def store_mid(j, value):
            mid[j] = value

        one_pass(src, store_mid, 10 * half, 10 + 8 * half, u, v, 1, width)
        one_pass(mid, store, 8 * half, 8 + 8 * half, u, v, 2, width)

    def exchange(n, rows=slice(None), lanes=slice(None), sem=0):
        pltpu.make_async_copy(
            asend.at[n, me, rows, lanes], arecv.at[n, me, rows, lanes], a_r.at[n, sem]
        ).start()

        @pl.loop(1, rows_n)
        def _(s):
            other = lax.rem(me + s, rows_n)
            pltpu.make_async_remote_copy(
                src_ref=asend.at[n, other, rows, lanes],
                dst_ref=arecv.at[n, me, rows, lanes],
                send_sem=a_s.at[n],
                recv_sem=a_r.at[n, sem],
                device_id={"rows": other},
                device_id_type=MESH,
            ).start()

    def arrived(n, lanes=slice(None), sem=0):
        blocks = arecv.at[n, :, :, lanes]
        pltpu.make_async_copy(blocks, blocks, a_r.at[n, sem]).wait()

    def sent(n):
        done = asend.at[n, pl.ds(0, rows_n - 1)]
        pltpu.make_async_copy(done, done, a_s.at[n]).wait()

    def load_pair(read):
        @pl.loop(0, 8, unroll=4)
        def _(i):
            x = read(i)
            high, low = split(x)
            pair[pl.ds(pl.multiple_of(16 * i, 16), 16), :] = high
            pair[pl.ds(pl.multiple_of(128 + 16 * i, 16), 16), :] = low

    def times_table(store):
        @pl.loop(0, width // tile, unroll=2)
        def _(n):
            cols = pl.ds(pl.multiple_of(n * tile, tile), tile)
            both = dot(pair[...], txh[:, cols])
            store(n, cols, both[:128] + both[128:] + dot(pair[pl.ds(0, 128), :], txl[:, cols]))

    def to_columns(n):
        def store(t, cols, value):
            for h in range(tile // 128):
                freq[t * (tile // 128) + h] = value[:, 128 * h : 128 * h + 128]

        times_table(store)

        @pl.loop(0, groups, unroll=4)
        def _(g):
            for h in range(2):
                tiles = [freq[g, pl.ds(4 * h + i, ROW, stride=LEV), :] for i in range(4)]
                for j, t in enumerate(swap_blocks(tiles)):
                    asend[n, 4 * g + j, :, 128 * h : 128 * h + 128] = t

    def half_to_columns(n, read, half):
        @pl.loop(0, 4, unroll=4)
        def _(i):
            high, low = split(read(4 * half + i))
            pair[pl.ds(pl.multiple_of(128 * half + 16 * i, 16), 16), :] = high
            pair[pl.ds(pl.multiple_of(128 * half + 64 + 16 * i, 16), 16), :] = low

        @pl.loop(0, width // tile, unroll=2)
        def _(t):
            cols = pl.ds(pl.multiple_of(t * tile, tile), tile)
            both = dot(pair[pl.ds(128 * half, 128), :], txh[:, cols])
            value = both[:64] + both[64:] + dot(pair[pl.ds(128 * half, 64), :], txl[:, cols])
            for h in range(tile // 128):
                freq[t * (tile // 128) + h, pl.ds(64 * half, 64)] = value[:, 128 * h : 128 * h + 128]

        @pl.loop(0, groups, unroll=4)
        def _(g):
            for h in range(2):
                tiles = [freq[g, pl.ds(64 * half + 4 * h + i, 8, stride=LEV), :] for i in range(4)]
                for j, t in enumerate(swap_blocks(tiles)):
                    asend[n, 4 * g + j, 8 * half : 8 * half + 8, 128 * h : 128 * h + 128] = t

        exchange(n, pl.ds(8 * half, 8))

    def from_columns(n, dst):
        for h in range(2):
            lanes = pl.ds(128 * h, 128)
            arrived(n, lanes, h)

            @pl.loop(0, groups, unroll=4)
            def _(g):
                tiles = [arecv[n, 4 * g + j, :, lanes] for j in range(4)]
                for i, t in enumerate(swap_blocks(tiles)):
                    freq[g, pl.ds(4 * h + i, ROW, stride=LEV), :] = t

        for g in range(groups):
            high, low = split(freq[g])
            pair[pl.ds(0, 128), 128 * g : 128 * g + 128] = high
            pair[pl.ds(128, 128), 128 * g : 128 * g + 128] = low

        def store(t, cols, value):
            dst[:, cols] = value

        times_table(store)

    def y_pair(h, read):
        @pl.loop(0, tall // 64, unroll=4)
        def _(i):
            rows = pl.ds(pl.multiple_of(64 * i, 64), 64)
            high, low = split(read(i, rows, pl.ds(128 * h, 128)))
            ypair[rows, 256 * h : 256 * h + 128] = high
            ypair[rows, 256 * h + 128 : 256 * h + 256] = low

    def y_times(h, store):
        @pl.loop(0, tall // ytile, unroll=2)
        def _(i):
            rows = pl.ds(pl.multiple_of(i * ytile, ytile), ytile)
            both = dot(tyh[rows, :], ypair[:, 256 * h : 256 * h + 256])
            low = dot(tyl[rows, :], ypair[:, 256 * h : 256 * h + 128])
            store(i, rows, pl.ds(128 * h, 128), both[:, 0:128] + both[:, 128:256] + low)

    def filter_rows(came, goes, store, read):
        def read_came(i, rows, lanes):
            return arecv[came, pl.ds(4 * i, 4), :, lanes].reshape(64, 128)

        def store_back(i, rows, lanes, value):
            count = ytile // ROW
            asend[goes, pl.ds(i * count, count), :, lanes] = value.reshape(count, ROW, 128)

        arrived(came)
        for h in range(2):
            y_pair(h, read_came)
            y_times(h, store)
            y_pair(h, read)
            y_times(h, store_back)
            exchange(goes, slice(None), pl.ds(128 * h, 128), h)

    def read_m(i):
        return pm[pl.ds(2 * i, 2)].reshape(16, width)

    loads[0].wait()
    regroup(mult_v, pm, 0)
    load_pair(read_m)
    loads[1].wait()
    loads[2].wait()
    to_columns(0)
    loads[3].wait()
    regroup(wind_v, pw, 2)
    loads[4].wait()
    regroup(inc_v, pi, 0)

    pl.semaphore_wait(barrier, rows_n - 1 + tm_n - 1)
    halos_w = halo(pw, 0)
    exchange(0)
    shift(pi, xi, 0, after)

    cells = cells_ref[...]
    n_obs = cells.shape[1]
    obs_row = cells // width
    obs_col = lax.rem(cells, width)

    @pl.loop(0, width // 128, unroll=2)
    def _(i):
        base = pl.multiple_of(128 * i, 128)
        at = lax.broadcasted_iota(jnp.int32, (128, n_obs), 0) + base
        onehot[pl.ds(base, 128), :] = jnp.where(at == obs_col, 1.0, 0.0).astype(BF16)

    def gather():
        both = dot(pair[...], onehot[...])
        picked = both[:128] + both[128:]
        total = jnp.zeros((LEV, n_obs), F32)
        for r in range(ROW):
            total = total + jnp.where(obs_row == r, picked[LEV * r : LEV * r + LEV], 0.0)
        return total

    def scatter(values, store):
        for r in range(0, ROW, 2):
            x = jnp.concatenate(
                [jnp.where(obs_row == r, values, 0.0), jnp.where(obs_row == r + 1, values, 0.0)], axis=0
            )
            high, low = split(x)
            wpair[pl.ds(LEV * r, 16), :] = high
            wpair[pl.ds(128 + LEV * r, 16), :] = low

        @pl.loop(0, width // tile, unroll=2)
        def _(n):
            cols = pl.ds(pl.multiple_of(n * tile, tile), tile)
            both = dot_t(wpair[...], onehot[cols, :])
            store(cols, (both[:128] + both[128:]).reshape(ROW, LEV, tile))

    def read_i(i):
        return pi[pl.ds(2 * i, 2)].reshape(16, width)

    load_pair(read_i)
    weighted = weight_ref[...] * (obs_ref[...] - gather())

    def store_d(cols, value):
        pd[:, :, cols] = value - pm[:, :, cols]

    scatter(weighted, store_d)
    shift(pm, xm, 1, before)

    loads[5].wait()

    @pl.loop(0, ROW, unroll=4)
    def _(r):
        for g in range(groups):
            lanes = slice(128 * g, 128 * g + 128)
            q0[r, :, lanes] = misfit_v[g, pl.ds(r, LEV, stride=ROW), :] - pi[r, :, lanes]

    loads[6].wait()

    @pl.loop(0, tall // 128, unroll=2)
    def _(i):
        rows = pl.ds(pl.multiple_of(128 * i, 128), 128)
        for h in range(2):
            lanes = slice(128 * h, 128 * h + 128)
            spec[rows, lanes] = spec_v[lanes, rows].T

    whole = 1.0 / (width * tall)

    level = lax.broadcasted_iota(jnp.int32, (LEV, 1), 0)

    def picks(section):
        column = jnp.zeros((LEV, 1), jnp.int32)
        for l in range(LEV):
            column = jnp.where(level == l, choice_ref[section, l], column)
        return [jnp.broadcast_to(column == n, (LEV, width)) for n in range(4)]

    for copy in halos_w:
        copy.wait_recv()

    @pl.loop(0, ROW + 4, unroll=2)
    def _(r):
        half = 0.5 * pw[r]
        for section, u_ref, v_ref in ((sec, own_u, own_v), (before, prev_u, prev_v)):
            chosen = picks(section)
            for comp, ref in ((0, u_ref), (1, v_ref)):
                value = jnp.zeros((LEV, width), F32)
                for n in range(4):
                    row = jnp.broadcast_to(half[2 * n + comp : 2 * n + comp + 1], (LEV, width))
                    value = jnp.where(chosen[n], row, value)
                ref[r] = value

    halos_i = edges(xi, 0)
    halos_m = edges(xm, 1)

    loads[7].wait()
    loads[8].wait()

    def store_sm(i, rows, lanes, value):
        smul[rows, lanes] = spec[rows, lanes] * value

    def read_sm(i, rows, lanes):
        return smul[rows, lanes] * whole

    filter_rows(0, 1, store_sm, read_sm)

    keep_back = jnp.where(sec < tm_n - 1, 1.0, 0.0)
    keep_front = jnp.where(sec > 0, 1.0, 0.0)

    def store_q(j, value):
        q0[j] = q0[j] + keep_front * value

    def read_q(i):
        return q0[pl.ds(2 * i, 2)].reshape(16, width)

    front(xi, 0, halos_i)
    twice(forward_pass, xi, store_q, prev_u, prev_v, 0)
    half_to_columns(2, read_q, 0)
    back(xi, 0)
    twice(forward_pass, xi, store_q, prev_u, prev_v, 1)
    half_to_columns(2, read_q, 1)

    def store_back(j, value):
        pd[j] = pd[j] + keep_back * value

    front(xm, 1, halos_m)
    twice(adjoint_pass, xm, store_back, own_u, own_v, 0)
    back(xm, 1)
    twice(adjoint_pass, xm, store_back, own_u, own_v, 1)
    shift(pd, xd, 2, after)

    from_columns(1, bfield)

    @pl.loop(0, ROW, unroll=4)
    def _(r):
        pr[r] = q0[r] - bfield[pl.ds(pl.multiple_of(LEV * r, LEV), LEV), :]

    shift(pr, xr, 3, before)

    def read_d(i):
        return pd[pl.ds(2 * i, 2)].reshape(16, width)

    load_pair(read_d)

    def store_f(cols, value):
        ffield[:, :, cols] = value

    scatter(weight_ref[...] * gather(), store_f)

    halos_d = edges(xd, 2)

    def store_rm(i, rows, lanes, value):
        smul[rows, lanes] = spec[rows, lanes] * (value - smul[rows, lanes]) * whole

    def read_rm(i, rows, lanes):
        return smul[rows, lanes]

    filter_rows(2, 3, store_rm, read_rm)

    halos_r = edges(xr, 3)

    def store_e(j, value):
        efield[j] = keep_front * value - pd[j]

    def store_k(j, value):
        kfield[j] = keep_back * value - pr[j]

    front(xd, 2, halos_d)
    twice(forward_pass, xd, store_e, prev_u, prev_v, 0)
    back(xd, 2)
    twice(forward_pass, xd, store_e, prev_u, prev_v, 1)
    front(xr, 3, halos_r)
    twice(adjoint_pass, xr, store_k, own_u, own_v, 0)
    from_columns(3, bfield)
    back(xr, 3)
    twice(adjoint_pass, xr, store_k, own_u, own_v, 1)

    def fold(x):
        total = x[:, 0:128]
        for g in range(1, groups):
            total = total + x[:, 128 * g : 128 * g + 128]
        return total

    def inner(count, pairs_of):
        def step(r, sums):
            return tuple(s + fold(x * y) for s, (x, y) in zip(sums, pairs_of(r)))

        return lax.fori_loop(0, ROW, step, (jnp.zeros((LEV, 128), F32),) * count, unroll=2)

    def pairs_early(r):
        a, d, e, f, k = pr[r], pd[r], efield[r], ffield[r], kfield[r]
        return (a, a), (e, e), (a, e), (d, d), (f, f), (k, k), (d, f), (d, k), (f, k)

    early = inner(9, pairs_early)

    def filtered(r):
        return bfield[pl.ds(pl.multiple_of(LEV * r, LEV), LEV), :]

    def pairs_late(r):
        b = filtered(r)
        return (b, b), (pr[r], b), (b, efield[r])

    late = inner(3, pairs_late)
    lane = lax.broadcasted_iota(jnp.int32, (1, 128), 1)
    row = jnp.zeros((1, 128), F32)
    for n, value in enumerate(early + late):
        one = jnp.sum(jnp.sum(value, axis=0, keepdims=True), axis=1, keepdims=True)
        row = jnp.where(lane == n, one, row)
    part[...] = row

    def everywhere(own, slots, axis, here, count, n):
        pltpu.make_async_copy(own, slots.at[here], sum_r.at[n]).start()

        @pl.loop(1, count)
        def _(s):
            pltpu.make_async_remote_copy(
                src_ref=own,
                dst_ref=slots.at[here],
                send_sem=sum_s.at[n],
                recv_sem=sum_r.at[n],
                device_id={axis: lax.rem(here + s, count)},
                device_id_type=MESH,
            ).start()

        pltpu.make_async_copy(slots, slots, sum_r.at[n]).wait()
        return jnp.sum(slots[...], axis=0)

    part2[...] = everywhere(part, zsum, "tm", sec, tm_n, 0)
    total = everywhere(part2, rsum, "rows", me, rows_n, 1)
    aa, ee, ae, dd, ff, kk, df, dk, fk, bb, ab, be = (total[:, n : n + 1] for n in range(12))
    t0 = aa / (aa + dd + 1e-6)
    s0 = 1.0 - t0
    lam = aa + t0 * t0 * bb + s0 * s0 * ee + 2.0 * (s0 * ae - t0 * ab - t0 * s0 * be)
    dx = dd + s0 * s0 * ff + t0 * t0 * kk + 2.0 * (t0 * dk - s0 * df - t0 * s0 * fk)
    lam = jnp.maximum(lam, 0.0)
    dx = jnp.maximum(dx, 0.0)
    t1 = lam / (lam + dx + 1e-6)
    s1 = 1.0 - t1

    @pl.loop(0, ROW, unroll=4)
    def _(r):
        a, b, d, e, f, k = pr[r], filtered(r), pd[r], efield[r], ffield[r], kfield[r]
        x = pm[r] + t0 * a + t1 * (a - t0 * b + s0 * e)
        y = pi[r] + s0 * d + s1 * (d - s0 * f + t0 * k)
        for g in range(groups):
            lanes = slice(128 * g, 128 * g + 128)
            mult_v[g, pl.ds(r, LEV, stride=ROW), :] = x[:, lanes]
            inc_v[g, pl.ds(r, LEV, stride=ROW), :] = y[:, lanes]

    for g in range(groups):
        lanes = slice(128 * g, 128 * g + 128)
        mult_out[:, lanes] = mult_v[g]
        inc_out[:, lanes] = inc_v[g]

    for copies in (halos_w, halos_i, halos_m, halos_d, halos_r):
        for copy in copies:
            copy.wait_send()
    for n, src in enumerate((pi, pm, pd, pr)):
        pltpu.make_async_copy(src, src, z_s.at[n]).wait()
    for n in range(4):
        sent(n)
    gone = zsum.at[pl.ds(0, tm_n - 1)]
    pltpu.make_async_copy(gone, gone, sum_s.at[0]).wait()
    gone = rsum.at[pl.ds(0, rows_n - 1)]
    pltpu.make_async_copy(gone, gone, sum_s.at[1]).wait()


def solution(mesh):
    rows_n = mesh.shape["rows"]
    tm_n = mesh.shape["tm"]
    width = COL * rows_n
    tall = ROW * rows_n
    x_tables = cas_pair(width)
    y_tables = cas_pair(tall)

    def on_device(misfit, mult, inc, obs, weights, cells, wind, choice, spectrum):
        n_obs = cells.shape[1]
        field = (LEV * ROW, width)
        padded = (ROW + 4, LEV, width)
        lanes = (width // 128, LEV * ROW, 128)
        vm = pltpu.VMEM
        dma = pltpu.SemaphoreType.DMA
        scratch = [
            vm(lanes, F32),
            vm(lanes, F32),
            vm(lanes, F32),
            vm(lanes, F32),
            vm((LEV * COL, tall), F32),
            vm((width, width), BF16),
            vm((width, width), BF16),
            vm((tall, tall), BF16),
            vm((tall, tall), BF16),
        ]
        inner = (ROW, LEV, width)
        scratch += [vm(inner, F32)] * 2 + [vm(padded, F32)] + [vm(inner, F32)] * 2
        scratch += [vm(padded, F32)] * 4
        scratch += [
            vm((ROW + 2, LEV, width), F32),
            vm(inner, F32),
        ]
        scratch += [vm(padded, F32)] * 4 + [vm(inner, F32)] * 2
        scratch += [
            vm((4, rows_n, ROW, LEV * COL), F32),
            vm((4, rows_n, ROW, LEV * COL), F32),
            vm((width // 128, 128, 128), F32),
            vm((256, width), BF16),
            vm((tall, 512), BF16),
            vm((tall, 256), F32),
            vm((tall, 256), F32),
            vm((width, n_obs), BF16),
            vm((256, n_obs), BF16),
            vm(field, F32),
            vm((ROW, LEV, width), F32),
            vm((1, 128), F32),
            vm((1, 128), F32),
            vm((tm_n, 1, 128), F32),
            vm((rows_n, 1, 128), F32),
            dma((9,)),
            dma((10,)),
            dma((10,)),
            dma((4,)),
            dma((4, 3)),
            dma((4,)),
            dma((4, 2)),
            dma((2,)),
            dma((2,)),
        ]
        anywhere = pl.BlockSpec(memory_space=pl.ANY)
        near = pl.BlockSpec(memory_space=pltpu.VMEM)
        outs = pl.pallas_call(
            functools.partial(kernel, rows_n, tm_n),
            out_shape=(pltpu.VMEM(field, F32),) * 2,
            in_specs=[
                anywhere,
                anywhere,
                anywhere,
                near,
                near,
                near,
                anywhere,
                pl.BlockSpec(memory_space=pltpu.SMEM),
                anywhere,
                anywhere,
                anywhere,
                anywhere,
                anywhere,
            ],
            out_specs=(near, near),
            scratch_shapes=scratch,
            compiler_params=pltpu.CompilerParams(
                collective_id=0, has_side_effects=True, vmem_limit_bytes=56 * 1024 * 1024
            ),
            name="saddle",
        )(
            misfit.reshape(field),
            mult.reshape(field),
            inc.reshape(field),
            obs[0],
            weights[0],
            cells,
            wind.reshape(field),
            choice,
            jnp.transpose(spectrum, (0, 2, 1)).reshape(LEV * COL, tall),
            *(jnp.asarray(t) for t in x_tables),
            *(jnp.asarray(t) for t in y_tables),
        )
        return tuple(o.reshape(1, LEV, ROW, width) for o in outs)

    return jax.shard_map(
        on_device,
        mesh=mesh,
        in_specs=(
            P("tm", None, "rows", None),
            P("tm", None, "rows", None),
            P("tm", None, "rows", None),
            P("tm", None, "rows"),
            P("tm", None, "rows"),
            P("tm", "rows"),
            P(None, None, "rows", None),
            P(),
            P(None, None, "rows"),
        ),
        out_specs=(P("tm", None, "rows", None), P("tm", None, "rows", None)),
        check_vma=False,
    )
```
